512 devices in a mesh: tensor: 8 (over x, core), context: 64 (over z, y).
Axes of the slice: x: 4, y: 4, z: 16, core: 2. Of those that a mesh axis runs over, the one named last changes fastest.
Arguments:
- features: bfloat16 [3, 8192, 4096], P(None, 'context', 'tensor'), may hold values from -6 to 6
- short_filter: float32 [3, 3, 4096], P(None, None, 'tensor'), may hold values from -3 to 3
- long_filter: bfloat16 [8192, 4096], P('context', 'tensor'), may hold values from -1 to 1
- skip_gain: float32 [4096], P('tensor'), may hold values from -4 to 4
- norm_gain: float32 [4096], P('tensor'), may hold values from 0.1 to 1.9
- out_grad: bfloat16 [8192, 4096], P('context', 'tensor'), may hold values from -6 to 6
Outputs:
- layer_out: bfloat16 [8192, 4096], P('context', 'tensor')
- feature_grad: float32 [3, 8192, 4096], P(None, 'context', 'tensor')
- filter_grad: float32 [8192, 4096], P('context', 'tensor')
The draws below stay inside these ranges and needn't reach their ends.
All inputs are finite; a program needn't handle non-finite values.
Results may differ from the reference program's by a relative error of at most 0.005.
Values sent between devices are 32-bit elements; how exact they have to be, the bound alone decides.
A program may use at most 64 MiB of HBM per device.

```python
import math
import jax
import jax.numpy as jnp
from jax import lax

CHANNELS = 4096
SHORT = 3
SEQ = 8192


def draw_skip_gain(key, part):
    key = jax.random.fold_in(key, 11)
    sign_key, size_key = jax.random.split(key)
    where = jnp.arange(CHANNELS, dtype=jnp.float32) / max(CHANNELS - 1, 1)
    level = 0.3 + 2.7 * where
    jitter = jax.random.uniform(size_key, (CHANNELS,), jnp.float32, 0.8, 1.2)
    signs = jnp.where(jax.random.bernoulli(sign_key, 0.5, (CHANNELS,)), 1.0, -1.0)
    return (level * jitter * signs).astype(jnp.float32)


def draw_long_filter(key, part):
    key = jax.random.fold_in(key, 23)
    rough_key = jax.random.fold_in(key, 0)
    factor = 1.2 / math.sqrt(SEQ)
    values = factor * jnp.clip(jax.random.normal(rough_key, (SEQ, CHANNELS), jnp.float32), -6.0, 6.0)
    return values.astype(jnp.bfloat16)


def steps_of(key, shape, pieces, smallest, largest):
    level = 1.0
    for position, blocks in pieces:
        steps = jax.random.uniform(jax.random.fold_in(jax.random.fold_in(key, 6), position), (blocks,), jnp.float32, smallest / len(pieces), largest / len(pieces))
        level = level * jnp.repeat(jnp.exp(steps), shape[position] // blocks).reshape((-1,) + (1,) * (len(shape) - 1 - position))
    return level


def bell_draw(stream_key, shape, deviation, most, cuts=(), held_as=jnp.bfloat16):
    gain = steps_of(stream_key, shape, cuts, -0.22, 0.18) if cuts else 1.0
    entries = jax.random.normal(stream_key, shape, jnp.float32) * deviation * gain
    return jnp.minimum(jnp.maximum(entries, -most), most).astype(held_as)


def setup_inputs(seed: int = 0) -> dict:
    key_list = jax.random.split(jax.random.key(seed), 7)
    return {
        "features": bell_draw(key_list[0], (3, SEQ, CHANNELS), 1.0, 6.0, ((1, 64), (2, 8))),
        "short_filter": bell_draw(key_list[1], (3, SHORT, CHANNELS), 0.6, 3.0, ((2, 8),), jnp.float32),
        "long_filter": draw_long_filter(jax.random.fold_in(key_list[6], 71), 0),
        "skip_gain": draw_skip_gain(jax.random.fold_in(key_list[6], 71), 0),
        "norm_gain": jnp.clip(1.0 + 0.18 * jax.random.normal(key_list[4], (CHANNELS,), jnp.float32), 0.1, 1.9),
        "out_grad": bell_draw(key_list[5], (SEQ, CHANNELS), 1.0, 6.0, ((0, 64), (1, 8))),
    }


eps = 1e-06

def rounded_copy(values):
    return lax.optimization_barrier(values.astype(jnp.bfloat16)).astype(jnp.float32)

def spectral_product(left, right, conjugate):
    positions, channels = left.shape
    length = 2 * positions
    width = 512 if channels % 512 == 0 else channels
    groups = channels // width
    left_blocks = left.reshape(positions, groups, width).transpose(1, 0, 2)
    right_blocks = right.reshape(positions, groups, width).transpose(1, 0, 2)

    def one_block(blocks_pair):
        left_part, right_part = blocks_pair
        left_freq = jnp.fft.rfft(left_part, n=length, axis=0)
        right_freq = jnp.fft.rfft(right_part, n=length, axis=0)
        if conjugate:
            right_freq = jnp.conj(right_freq)
        return jnp.fft.irfft(left_freq * right_freq, n=length, axis=0)[:positions]
    result = lax.map(one_block, (left_blocks, right_blocks))
    return result.transpose(1, 0, 2).reshape(positions, channels).astype(left.dtype)

def reference(features, short_filter, long_filter, skip_gain, norm_gain, out_grad):
    tap_count = short_filter.shape[1]
    margin = tap_count - 1
    inputs = jnp.pad(features.astype(jnp.float32), ((0, 0), (margin, 0), (0, 0)))
    branches = jnp.zeros(features.shape, jnp.float32)
    for offset in range(tap_count):
        branches = branches + short_filter[:, offset, None, :] * inputs[:, margin - offset:margin - offset + SEQ, :]
    queries, key_part, value_part = (branches[0], branches[1], branches[2])
    mixed = rounded_copy(key_part * value_part)
    filters = long_filter.astype(jnp.float32)
    conved = spectral_product(filters, mixed, False)
    inner = conved + skip_gain * mixed
    gated = queries * inner
    scale = lax.rsqrt(lax.optimization_barrier(jnp.sum(gated * gated, axis=-1, keepdims=True)) / CHANNELS + eps)
    layer_out = (gated * scale * norm_gain).astype(jnp.bfloat16)
    scaled = out_grad.astype(jnp.float32) * norm_gain
    moment = lax.optimization_barrier(jnp.sum(scaled * gated, axis=-1, keepdims=True)) / CHANNELS
    d_gated = scale * scaled - gated * scale ** 3 * moment
    d_conv = d_gated * queries
    conv_grad = rounded_copy(d_conv)
    d_query = d_gated * inner
    back = spectral_product(conv_grad, filters, True)
    filter_grad = spectral_product(conv_grad, mixed, True)
    d_mixed = back + skip_gain * d_conv
    d_branch = jnp.stack([d_query, d_mixed * value_part, d_mixed * key_part])
    padded_grads = jnp.pad(d_branch, ((0, 0), (0, margin), (0, 0)))
    feature_grad = jnp.zeros(features.shape, jnp.float32)
    for offset in range(tap_count):
        feature_grad = feature_grad + short_filter[:, offset, None, :] * padded_grads[:, offset:offset + SEQ, :]
    return (layer_out, feature_grad, filter_grad)
```

```python
import functools

import jax
import jax.numpy as jnp
import numpy as np
from jax import lax
from jax.sharding import PartitionSpec as P

CHANNELS = 4096
EPS = 1e-06


def constants(blocks, width):
    length = 2 * blocks * width
    doubled = 2 * blocks
    a = np.arange(blocks)
    k1 = np.arange(blocks) + 0.5
    first = 2.0 * np.pi * k1[:, None] * a[None, :] / doubled
    f1 = np.concatenate([np.cos(first), -np.sin(first)], axis=0)
    g1 = np.concatenate([np.cos(first.T), -np.sin(first.T)], axis=1) * (2.0 / length)
    b = np.arange(width)
    twist = 2.0 * np.pi * k1[:, None] * b[None, :] / length
    second = 2.0 * np.pi * ((b[:, None] * b[None, :]) % width) / width
    c, s = np.cos(second), np.sin(second)
    f2 = np.block([[c, -s], [s, c]])
    g2 = np.block([[c, s], [-s, c]])
    return [x.astype(np.float32) for x in (f1, f2, g1, g2, np.cos(twist), np.sin(twist))]


def mm(spec, a, b):
    return jnp.einsum(spec, a, b, precision=lax.Precision.HIGHEST, preferred_element_type=jnp.float32)


def forward(x, consts):
    f1, f2, _, _, wr, wi = consts
    blocks = x.shape[1]
    z = mm("ka,sacb->sckb", f1, x)
    re, im = z[:, :, :blocks], z[:, :, blocks:]
    t = jnp.concatenate([re * wr + im * wi, im * wr - re * wi], axis=-1)
    return mm("sckb,bn->sckn", t, f2)


def inverse(spec, consts):
    _, _, g1, g2, wr, wi = consts
    width = spec.shape[-1] // 2
    t = mm("sckn,nb->sckb", spec, g2)
    re, im = t[..., :width], t[..., width:]
    u = jnp.concatenate([re * wr - im * wi, im * wr + re * wi], axis=2)
    return mm("ak,sckb->sacb", g1, u)


def times(p, q, conj):
    w = p.shape[-1] // 2
    pr, pi, qr, qi = p[..., :w], p[..., w:], q[..., :w], q[..., w:]
    if conj:
        qi = -qi
    return jnp.concatenate([pr * qr - pi * qi, pr * qi + pi * qr], axis=-1)


def to_columns(fields):
    n = lax.axis_size("context")
    s, rows, channels = fields.shape
    parts = jnp.swapaxes(fields, 1, 2).reshape(s, n, channels // n, rows)
    return lax.all_to_all(parts, "context", split_axis=1, concat_axis=1, tiled=True)


def to_rows(cols):
    s, n, ch, rows = cols.shape
    back = lax.all_to_all(cols, "context", split_axis=1, concat_axis=1, tiled=True)
    return jnp.swapaxes(back.reshape(s, n * ch, rows), 1, 2)


def rounded_copy(values):
    return lax.optimization_barrier(values.astype(jnp.bfloat16)).astype(jnp.float32)


def channel_total(values):
    return lax.psum(jnp.sum(values, axis=-1), "tensor")


def neighbour_rows(block, by):
    size = lax.axis_size("context")
    pairs = [(i, i + by) for i in range(size) if 0 <= i + by < size]
    return lax.ppermute(block, "context", pairs)


def per_device(features, short_filter, long_filter, skip_gain, norm_gain, out_grad):
    taps = short_filter.shape[1]
    margin = taps - 1
    rows = features.shape[1]
    consts = constants(lax.axis_size("context"), rows)
    inputs = features.astype(jnp.float32)
    previous = neighbour_rows(inputs[:, rows - margin :, :], 1)
    extended = jnp.concatenate([previous, inputs], axis=1)
    branches = sum(
        short_filter[:, j, None, :] * extended[:, margin - j : margin - j + rows, :]
        for j in range(taps)
    )
    queries, key_part, value_part = branches[0], branches[1], branches[2]
    filters = long_filter.astype(jnp.float32)
    incoming = out_grad.astype(jnp.float32)
    mixed = rounded_copy(key_part * value_part)
    specs = forward(to_columns(jnp.stack([mixed, filters])), consts)
    mixed_s, filter_s = specs[0:1], specs[1:2]
    conved = to_rows(inverse(times(mixed_s, filter_s, False), consts))[0]
    inner = conved + skip_gain * mixed
    gated = queries * inner
    scaled = incoming * norm_gain
    sums = lax.psum(
        jnp.stack([jnp.sum(gated * gated, axis=-1), jnp.sum(scaled * gated, axis=-1)]), "tensor"
    )
    scale = lax.rsqrt(sums[0] / CHANNELS + EPS)[:, None]
    moment = (sums[1] / CHANNELS)[:, None]
    layer_out = (gated * scale * norm_gain).astype(jnp.bfloat16)
    d_gated = scale * scaled - gated * scale**3 * moment
    d_conv = d_gated * queries
    d_query = d_gated * inner
    grad_s = forward(to_columns(rounded_copy(d_conv)[None]), consts)
    pair = to_rows(
        inverse(jnp.concatenate([times(grad_s, filter_s, True), times(grad_s, mixed_s, True)]), consts)
    )
    back, filter_grad = pair[0], pair[1]
    d_mixed = back + skip_gain * d_conv
    d_branch = jnp.stack([d_query, d_mixed * value_part, d_mixed * key_part])
    later = neighbour_rows(d_branch[:, :margin, :], -1)
    padded = jnp.concatenate([d_branch, later], axis=1)
    feature_grad = sum(
        short_filter[:, j, None, :] * padded[:, j : j + rows, :] for j in range(taps)
    )
    return (layer_out, feature_grad, filter_grad)


def solution(mesh):
    return jax.shard_map(
        per_device,
        mesh=mesh,
        in_specs=(
            P(None, "context", "tensor"),
            P(None, None, "tensor"),
            P("context", "tensor"),
            P("tensor"),
            P("tensor"),
            P("context", "tensor"),
        ),
        out_specs=(P("context", "tensor"), P(None, "context", "tensor"), P("context", "tensor")),
        check_vma=False,
    )
```

```python
import functools

import jax
import jax.numpy as jnp
import ml_dtypes
import numpy as np
from jax import lax
from jax.experimental import pallas as pl
from jax.experimental.pallas import tpu as pltpu
from jax.sharding import PartitionSpec as P

CHANNELS = 4096
EPS = 1e-06
F32 = jnp.float32
BF16 = jnp.bfloat16
MESH = pl.DeviceIdType.MESH
RING = 16
SIDE = 4
LANES = 128
CH = 8


def constants(blocks, width):
    length = 2 * blocks * width
    a = np.arange(blocks)
    k1 = np.arange(blocks) + 0.5
    first = 2.0 * np.pi * k1[:, None] * a[None, :] / (2 * blocks)
    f1 = np.concatenate([np.cos(first), -np.sin(first)], axis=0)
    g1 = np.concatenate([np.cos(first.T), -np.sin(first.T)], axis=1) * (2.0 / length)
    b = np.arange(width)
    twist = 2.0 * np.pi * k1[:, None] * b[None, :] / length
    second = 2.0 * np.pi * ((b[:, None] * b[None, :]) % width) / width
    c, s = np.cos(second), np.sin(second)
    f2 = np.block([[c, -s], [s, c]])
    g2 = np.block([[c, s], [-s, c]])

    def split(m):
        high = m.astype(ml_dtypes.bfloat16)
        low = (m - high.astype(np.float64)).astype(ml_dtypes.bfloat16)
        return high, low

    f1h, f1l = split(f1)
    f2h, f2l = split(f2)
    g1h, g1l = split(g1)
    g2h, g2l = split(g2)
    twists = [np.cos(twist).astype(np.float32), np.sin(twist).astype(np.float32)]
    return [np.concatenate([f1h, f1l], axis=0), f2h, f2l, g1h, g1l, g2h, g2l] + twists


def dot(a, b):
    return jnp.dot(a, b, preferred_element_type=F32)


def halves(x):
    high = x.astype(BF16)
    return high, (x - high.astype(F32)).astype(BF16)


def kernel(
    feat, taps, filt, skip, gain, grad,
    f1, f2h, f2l, g1h, g1l, g2h, g2l, wr, wi,
    out, fgrad, hgrad,
    send, recv, qt, kt, vt, mt, st, it, gt, ct, spec_h, spec_x, spec_g, th, tl, db,
    halo_s, halo_r, norm_s, norm_r,
    send_sem, recv_sem, halo_send, halo_recv, norm_send, norm_recv,
):
    me = lax.axis_index("context")
    lane = lax.axis_index("tensor")
    n_ctx = lax.axis_size("context")
    n_ten = lax.axis_size("tensor")
    my_z, my_y = me // SIDE, me % SIDE
    wide = LANES * SIDE
    chunks = [slice(j * LANES, (j + 1) * LANES) for j in range(wide // LANES)]

    def peer(i):
        k = i // SIDE
        odd = k % 2
        dz = odd * ((k + 1) // 2) + (1 - odd) * (RING - k // 2)
        return ((my_z + dz) % RING) * SIDE + (my_y + i % SIDE) % SIDE

    barrier = pltpu.get_barrier_semaphore()

    def greet(i, carry):
        pl.semaphore_signal(barrier, inc=1, device_id={"context": peer(i)}, device_id_type=MESH)
        return carry

    def greet_tensor(i, carry):
        pl.semaphore_signal(
            barrier, inc=1, device_id={"tensor": (lane + i) % n_ten}, device_id_type=MESH
        )
        return carry

    lax.fori_loop(1, n_ctx, greet, 0)
    lax.fori_loop(1, n_ten, greet_tensor, 0)

    def tile(i):
        return pl.ds(pl.multiple_of(i * CH, CH), CH)

    def scatter(u):
        pltpu.make_async_copy(send.at[u, tile(me)], recv.at[u, tile(me)], recv_sem.at[u]).start()

        def body(i, carry):
            p = peer(i)
            pltpu.make_async_remote_copy(
                src_ref=send.at[u, tile(p)],
                dst_ref=recv.at[u, tile(me)],
                send_sem=send_sem.at[u],
                recv_sem=recv_sem.at[u],
                device_id={"context": p},
                device_id_type=MESH,
            ).start()
            return carry

        lax.fori_loop(1, n_ctx, body, 0)

    def arrived(u):
        pltpu.make_async_copy(send.at[u], recv.at[u], recv_sem.at[u]).wait()

    def halo_copy(h, to):
        return pltpu.make_async_remote_copy(
            src_ref=halo_s.at[h],
            dst_ref=halo_r.at[h],
            send_sem=halo_send.at[h],
            recv_sem=halo_recv.at[h],
            device_id={"context": to},
            device_id_type=MESH,
        )

    for j, c in enumerate(chunks):
        send[0, c, :] = filt[:, c].astype(F32).T
    for i in range(3):
        halo_s[0, 2 * i : 2 * i + 2, :] = feat[i, 112:128, :].astype(F32)[14:16]
    halo_s[0, 6:8, :] = jnp.zeros((2, wide), F32)
    pl.semaphore_wait(barrier, n_ctx - 1 + n_ten - 1)

    first_halo = halo_copy(0, (me + 1) % n_ctx)
    first_halo.start()
    scatter(0)

    for j, c in enumerate(chunks):
        st[c, :] = (grad[:, c].astype(F32) * gain[0:1, c]).T
        gt[c, :] = jnp.broadcast_to(skip[0:1, c], (LANES, LANES)).T

    row = lax.broadcasted_iota(jnp.int32, (LANES, LANES), 0)
    first_halo.wait_recv()
    keep = (me > 0).astype(F32)
    for j, c in enumerate(chunks):
        parts = []
        for i in range(3):
            x = feat[i, :, c].astype(F32)
            far = halo_r[0, 2 * i : 2 * i + 1, c] * keep
            near = halo_r[0, 2 * i + 1 : 2 * i + 2, c] * keep
            x1 = jnp.where(row == 0, near, pltpu.roll(x, 1, 0))
            x2 = jnp.where(row == 0, far, jnp.where(row == 1, near, pltpu.roll(x, 2, 0)))
            parts.append(
                taps[3 * i : 3 * i + 1, c] * x
                + taps[3 * i + 1 : 3 * i + 2, c] * x1
                + taps[3 * i + 2 : 3 * i + 3, c] * x2
            )
        qt[c, :] = parts[0].T
        k, v = parts[1].T, parts[2].T
        kt[c, :] = k
        vt[c, :] = v
        send[1, c, :] = (k * v).astype(BF16).astype(F32)
    scatter(1)
    for j, c in enumerate(chunks):
        mt[c, :] = send[1, c, :]

    blocks = 64

    def forward(u, spec):
        for p in range(CH // 2):
            x = jnp.concatenate(
                [recv[u, pl.ds(2 * p + e, blocks, stride=CH), :] for e in range(2)], axis=1
            ).astype(BF16)
            z = dot(f1[...], x)
            z = z[: 2 * blocks] + z[2 * blocks :]
            for e in range(2):
                re = z[:blocks, e * LANES : (e + 1) * LANES]
                im = z[blocks:, e * LANES : (e + 1) * LANES]
                rows = slice((2 * p + e) * blocks, (2 * p + e + 1) * blocks)
                h, l = halves(re * wr[...] + im * wi[...])
                th[rows, :LANES] = h
                tl[rows, :LANES] = l
                h, l = halves(im * wr[...] - re * wi[...])
                th[rows, LANES:] = h
                tl[rows, LANES:] = l
        spec[...] = dot(th[...], f2h[...]) + dot(tl[...], f2h[...]) + dot(th[...], f2l[...])

    def inverse(a, b, sign, u):
        for p in range(CH // 2):
            rows = slice(2 * p * blocks, 2 * (p + 1) * blocks)
            ar, ai = a[rows, :LANES], a[rows, LANES:]
            br, bi = b[rows, :LANES], sign * b[rows, LANES:]
            h, l = halves(ar * br - ai * bi)
            th[rows, :LANES] = h
            tl[rows, :LANES] = l
            h, l = halves(ar * bi + ai * br)
            th[rows, LANES:] = h
            tl[rows, LANES:] = l
        t = dot(th[...], g2h[...]) + dot(tl[...], g2h[...]) + dot(th[...], g2l[...])
        for p in range(CH // 2):
            both = []
            for e in range(2):
                rows = slice((2 * p + e) * blocks, (2 * p + e + 1) * blocks)
                re, im = t[rows, :LANES], t[rows, LANES:]
                both.append(
                    jnp.concatenate(
                        [re * wr[...] - im * wi[...], im * wr[...] + re * wi[...]], axis=0
                    )
                )
            h, l = halves(jnp.concatenate(both, axis=1))
            y = dot(g1h[...], h) + dot(g1h[...], l) + dot(g1l[...], h)
            for e in range(2):
                send[u, pl.ds(2 * p + e, blocks, stride=CH), :] = y[:, e * LANES : (e + 1) * LANES]

    arrived(0)
    forward(0, spec_h)
    arrived(1)
    forward(1, spec_x)
    inverse(spec_x, spec_h, 1.0, 2)
    scatter(2)

    arrived(2)
    square = jnp.zeros((1, LANES), F32)
    cross = jnp.zeros((1, LANES), F32)
    for c in chunks:
        inner = recv[2, c, :] + gt[c, :] * mt[c, :]
        gated = qt[c, :] * inner
        it[c, :] = inner
        ct[c, :] = gated
        square = square + jnp.sum(gated * gated, axis=0, keepdims=True)
        cross = cross + jnp.sum(st[c, :] * gated, axis=0, keepdims=True)
    norm_s[...] = jnp.zeros((8, LANES), F32)
    norm_s[0:1, :] = square
    norm_s[1:2, :] = cross
    pltpu.make_async_copy(norm_s, norm_r.at[lane], norm_recv).start()

    def share(i, carry):
        pltpu.make_async_remote_copy(
            src_ref=norm_s,
            dst_ref=norm_r.at[lane],
            send_sem=norm_send,
            recv_sem=norm_recv,
            device_id={"tensor": (lane + i) % n_ten},
            device_id_type=MESH,
        ).start()
        return carry

    lax.fori_loop(1, n_ten, share, 0)
    pltpu.make_async_copy(norm_r, norm_r, norm_recv).wait()
    total = norm_r[0]
    for i in range(1, 8):
        total = total + norm_r[i]
    scale = lax.rsqrt(total[0:1] / CHANNELS + EPS)
    pull = scale * scale * scale * (total[1:2] / CHANNELS)
    for c in chunks:
        d_gated = scale * st[c, :] - ct[c, :] * pull
        d_conv = d_gated * qt[c, :]
        send[3, c, :] = d_conv.astype(BF16).astype(F32)
        gt[c, :] = gt[c, :] * d_conv
        it[c, :] = d_gated * it[c, :]
    scatter(3)
    for c in chunks:
        out[:, c] = ((ct[c, :] * scale).T * gain[0:1, c]).astype(BF16)
        db[0, :, c] = it[c, :].T

    arrived(3)
    forward(3, spec_g)
    inverse(spec_g, spec_h, -1.0, 4)
    scatter(4)
    inverse(spec_g, spec_x, -1.0, 5)
    scatter(5)

    arrived(4)
    for c in chunks:
        d_mixed = recv[4, c, :] + gt[c, :]
        db[1, :, c] = (d_mixed * vt[c, :]).T
        db[2, :, c] = (d_mixed * kt[c, :]).T
    for i in range(3):
        halo_s[1, 2 * i : 2 * i + 2, :] = db[i, 0:2, :]
    halo_s[1, 6:8, :] = jnp.zeros((2, wide), F32)
    last_halo = halo_copy(1, (me + n_ctx - 1) % n_ctx)
    last_halo.start()
    last_halo.wait_recv()
    keep = (me < n_ctx - 1).astype(F32)
    for c in chunks:
        for i in range(3):
            x = db[i, :, c]
            near = halo_r[1, 2 * i : 2 * i + 1, c] * keep
            far = halo_r[1, 2 * i + 1 : 2 * i + 2, c] * keep
            x1 = jnp.where(row == LANES - 1, near, pltpu.roll(x, LANES - 1, 0))
            x2 = jnp.where(
                row == LANES - 1,
                far,
                jnp.where(row == LANES - 2, near, pltpu.roll(x, LANES - 2, 0)),
            )
            fgrad[i, :, c] = (
                taps[3 * i : 3 * i + 1, c] * x
                + taps[3 * i + 1 : 3 * i + 2, c] * x1
                + taps[3 * i + 2 : 3 * i + 3, c] * x2
            )
    arrived(5)
    for c in chunks:
        hgrad[:, c] = recv[5, c, :].T

    for u in range(6):
        gone = pl.ds(0, (n_ctx - 1) * CH)
        pltpu.make_async_copy(send.at[u, gone], send.at[u, gone], send_sem.at[u]).wait()
    first_halo.wait_send()
    last_halo.wait_send()
    spent = pl.ds(0, n_ten - 1)
    pltpu.make_async_copy(norm_r.at[spent], norm_r.at[spent], norm_send).wait()


def per_device(features, short_filter, long_filter, skip_gain, norm_gain, out_grad):
    rows, wide = long_filter.shape
    vmem = pl.BlockSpec(memory_space=pltpu.VMEM)
    column = pltpu.VMEM((wide, rows), F32)
    spec = pltpu.VMEM((wide, 2 * rows), F32)
    half = pltpu.VMEM((wide, 2 * rows), BF16)
    consts = [jnp.asarray(x) for x in constants(64, rows)]
    out, fgrad, hgrad = pl.pallas_call(
        kernel,
        out_shape=(
            jax.ShapeDtypeStruct((rows, wide), BF16),
            jax.ShapeDtypeStruct((3, rows, wide), F32),
            jax.ShapeDtypeStruct((rows, wide), F32),
        ),
        in_specs=[vmem] * (6 + len(consts)),
        out_specs=[vmem] * 3,
        scratch_shapes=[
            pltpu.VMEM((6, wide, rows), F32),
            pltpu.VMEM((6, wide, rows), F32),
        ]
        + [column] * 8
        + [spec] * 3
        + [half] * 2
        + [
            pltpu.VMEM((3, rows, wide), F32),
            pltpu.VMEM((2, 8, wide), F32),
            pltpu.VMEM((2, 8, wide), F32),
            pltpu.VMEM((8, rows), F32),
            pltpu.VMEM((8, 8, rows), F32),
            pltpu.SemaphoreType.DMA((6,)),
            pltpu.SemaphoreType.DMA((6,)),
            pltpu.SemaphoreType.DMA((2,)),
            pltpu.SemaphoreType.DMA((2,)),
            pltpu.SemaphoreType.DMA,
            pltpu.SemaphoreType.DMA,
        ],
        compiler_params=pltpu.CompilerParams(
            collective_id=0, has_side_effects=True, vmem_limit_bytes=48 * 1024 * 1024
        ),
    )(
        features,
        short_filter.reshape(9, wide),
        long_filter,
        skip_gain.reshape(1, wide),
        norm_gain.reshape(1, wide),
        out_grad,
        *consts,
    )
    return out, fgrad, hgrad


def solution(mesh):
    return jax.shard_map(
        per_device,
        mesh=mesh,
        in_specs=(
            P(None, "context", "tensor"),
            P(None, None, "tensor"),
            P("context", "tensor"),
            P("tensor"),
            P("tensor"),
            P("context", "tensor"),
        ),
        out_specs=(P("context", "tensor"), P(None, "context", "tensor"), P("context", "tensor")),
        check_vma=False,
    )
```

```python
import functools

import jax
import jax.numpy as jnp
import numpy as np
from jax import lax
from jax.experimental import pallas as pl
from jax.experimental.pallas import tpu as pltpu
from jax.sharding import PartitionSpec as P

CHANNELS = 4096
EPS = 1e-06
F32 = jnp.float32
BF16 = jnp.bfloat16
MESH = pl.DeviceIdType.MESH
RING = 16
SIDE = 4
LANES = 128
CH = 8
N_IN = 7
VMEM_BYTES = 63 * 1024 * 1024


def constants(blocks, width):
    length = 2 * blocks * width
    a = np.arange(blocks)
    k1 = np.arange(blocks) + 0.5
    first = 2.0 * np.pi * k1[:, None] * a[None, :] / (2 * blocks)
    f1 = np.concatenate([np.cos(first), -np.sin(first)], axis=0)
    g1 = np.concatenate([np.cos(first.T), -np.sin(first.T)], axis=1) * (2.0 / length)
    b = np.arange(width)
    twist = 2.0 * np.pi * k1[:, None] * b[None, :] / length
    second = 2.0 * np.pi * ((b[:, None] * b[None, :]) % width) / width
    c, s = np.cos(second), np.sin(second)
    f2 = np.block([[c, -s], [s, c]])
    g2 = np.block([[c, s], [-s, c]])

    pack = np.zeros((6 * width, 2 * width), np.float32)
    pack[: 2 * width] = f2
    pack[2 * width : 4 * width] = g2
    pack[4 * width : 5 * width, :blocks] = f1
    pack[5 * width : 5 * width + blocks, :width] = g1
    pack[5 * width + blocks : 6 * width, :width] = np.cos(twist)
    pack[5 * width + blocks : 6 * width, width:] = np.sin(twist)
    return pack


def dot(a, b):
    return jnp.dot(a, b, preferred_element_type=F32)


def halves(x):
    high = x.astype(BF16)
    return high, (x - high.astype(F32)).astype(BF16)


def kernel(
    *refs,
):
    held, (out, fgrad, hgrad) = refs[:N_IN], refs[N_IN : N_IN + 3]
    (send, recv, qt, kt, vt, st, it, gt, ct, spec_h, spec_x, spec_g, th, tl, db,
     halo_s, halo_r, norm_s, norm_r,
     f1, f2h, f2l, g1h, g1l, g2h, g2l, wr, wi,
     send_sem, recv_sem, halo_send, halo_recv, norm_send, norm_recv, in_sem) = refs[N_IN + 3 : -N_IN]
    local = refs[-N_IN:]
    feat, taps, filt, skip, gain, grad, consts = local
    fetch = [
        pltpu.make_async_copy(held[i], local[i], in_sem.at[i]) for i in range(N_IN)
    ]
    early = (2, 0)
    late = [i for i in range(N_IN) if i not in early]
    for i in early:
        fetch[i].start()
    me = lax.axis_index("context")
    lane = lax.axis_index("tensor")
    n_ctx = lax.axis_size("context")
    n_ten = lax.axis_size("tensor")
    my_z, my_y = me // SIDE, me % SIDE
    wide = LANES * SIDE
    chunks = [slice(j * LANES, (j + 1) * LANES) for j in range(wide // LANES)]

    def peer(i):
        i = n_ctx - i
        k = i // SIDE
        odd = k % 2
        dz = odd * ((k + 1) // 2) + (1 - odd) * (RING - k // 2)
        return ((my_z + dz) % RING) * SIDE + (my_y + i % SIDE) % SIDE

    barrier = pltpu.get_barrier_semaphore()

    def greet(i, carry):
        pl.semaphore_signal(barrier, inc=1, device_id={"context": peer(i)}, device_id_type=MESH)
        return carry

    def greet_tensor(i, carry):
        pl.semaphore_signal(
            barrier, inc=1, device_id={"tensor": (lane + i) % n_ten}, device_id_type=MESH
        )
        return carry

    lax.fori_loop(1, n_ctx, greet, 0)
    lax.fori_loop(1, n_ten, greet_tensor, 0)
    for i in late:
        fetch[i].start()

    def tile(i):
        return pl.ds(pl.multiple_of(i * CH, CH), CH)

    def scatter(u):
        pltpu.make_async_copy(send.at[u, tile(me)], recv.at[u, tile(me)], recv_sem.at[u]).start()

        def body(i, carry):
            p = peer(i)
            pltpu.make_async_remote_copy(
                src_ref=send.at[u, tile(p)],
                dst_ref=recv.at[u, tile(me)],
                send_sem=send_sem.at[u],
                recv_sem=recv_sem.at[u],
                device_id={"context": p},
                device_id_type=MESH,
            ).start()
            return carry

        lax.fori_loop(1, n_ctx, body, 0)

    def arrived(u):
        pltpu.make_async_copy(send.at[u], recv.at[u], recv_sem.at[u]).wait()

    def halo_copy(h, to):
        return pltpu.make_async_remote_copy(
            src_ref=halo_s.at[h],
            dst_ref=halo_r.at[h],
            send_sem=halo_send.at[h],
            recv_sem=halo_recv.at[h],
            device_id={"context": to},
            device_id_type=MESH,
        )

    fetch[2].wait()
    for j, c in enumerate(chunks):
        send[0, c, :] = filt[:, c].astype(F32).T
    fetch[0].wait()
    for i in range(3):
        halo_s[0, 2 * i : 2 * i + 2, :] = feat[i, 112:128, :].astype(F32)[14:16]
    halo_s[0, 6:8, :] = jnp.zeros((2, wide), F32)
    pl.semaphore_wait(barrier, n_ctx - 1 + n_ten - 1)

    first_halo = halo_copy(0, (me + 1) % n_ctx)
    first_halo.start()
    scatter(0)
    for i in late:
        fetch[i].wait()
    f2h[...], f2l[...] = halves(consts[0:256, :])
    g2h[...], g2l[...] = halves(consts[256:512, :])
    f1[0:128, :], f1[128:256, :] = halves(consts[512:640, 0:64])
    g1h[...], g1l[...] = halves(consts[640:704, 0:128])
    wr[...] = consts[704:768, 0:128]
    wi[...] = consts[704:768, 128:256]

    for j, c in enumerate(chunks):
        st[c, :] = (grad[:, c].astype(F32) * gain[0:1, c]).T
        gt[c, :] = jnp.broadcast_to(skip[0:1, c], (LANES, LANES)).T

    row = lax.broadcasted_iota(jnp.int32, (LANES, LANES), 0)
    first_halo.wait_recv()
    keep = (me > 0).astype(F32)
    for j, c in enumerate(chunks):
        parts = []
        for i in range(3):
            x = feat[i, :, c].astype(F32)
            far = halo_r[0, 2 * i : 2 * i + 1, c] * keep
            near = halo_r[0, 2 * i + 1 : 2 * i + 2, c] * keep
            x1 = jnp.where(row == 0, near, pltpu.roll(x, 1, 0))
            x2 = jnp.where(row == 0, far, jnp.where(row == 1, near, pltpu.roll(x, 2, 0)))
            parts.append(
                taps[i, 0 : 1, c] * x
                + taps[i, 1 : 2, c] * x1
                + taps[i, 2 : 3, c] * x2
            )
        qt[c, :] = parts[0].T
        k, v = parts[1].T, parts[2].T
        kt[c, :] = k
        vt[c, :] = v
        send[1, c, :] = (k * v).astype(BF16).astype(F32)
    scatter(1)

    blocks = 64

    def forward(u, spec):
        for p in range(CH // 2):
            x = jnp.concatenate(
                [recv[u, pl.ds(2 * p + e, blocks, stride=CH), :] for e in range(2)], axis=1
            ).astype(BF16)
            z = dot(f1[...], x)
            z = z[: 2 * blocks] + z[2 * blocks :]
            for e in range(2):
                re = z[:blocks, e * LANES : (e + 1) * LANES]
                im = z[blocks:, e * LANES : (e + 1) * LANES]
                rows = slice((2 * p + e) * blocks, (2 * p + e + 1) * blocks)
                h, l = halves(re * wr[...] + im * wi[...])
                th[rows, :LANES] = h
                tl[rows, :LANES] = l
                h, l = halves(im * wr[...] - re * wi[...])
                th[rows, LANES:] = h
                tl[rows, LANES:] = l
        spec[...] = dot(th[...], f2h[...]) + dot(tl[...], f2h[...]) + dot(th[...], f2l[...])

    def inverse(a, b, sign, u):
        for p in range(CH // 2):
            rows = slice(2 * p * blocks, 2 * (p + 1) * blocks)
            ar, ai = a[rows, :LANES], a[rows, LANES:]
            br, bi = b[rows, :LANES], sign * b[rows, LANES:]
            h, l = halves(ar * br - ai * bi)
            th[rows, :LANES] = h
            tl[rows, :LANES] = l
            h, l = halves(ar * bi + ai * br)
            th[rows, LANES:] = h
            tl[rows, LANES:] = l
        t = dot(th[...], g2h[...]) + dot(tl[...], g2h[...]) + dot(th[...], g2l[...])
        for p in range(CH // 2):
            both = []
            for e in range(2):
                rows = slice((2 * p + e) * blocks, (2 * p + e + 1) * blocks)
                re, im = t[rows, :LANES], t[rows, LANES:]
                both.append(
                    jnp.concatenate(
                        [re * wr[...] - im * wi[...], im * wr[...] + re * wi[...]], axis=0
                    )
                )
            h, l = halves(jnp.concatenate(both, axis=1))
            y = dot(g1h[...], h) + dot(g1h[...], l) + dot(g1l[...], h)
            for e in range(2):
                send[u, pl.ds(2 * p + e, blocks, stride=CH), :] = y[:, e * LANES : (e + 1) * LANES]

    arrived(0)
    forward(0, spec_h)
    arrived(1)
    forward(1, spec_x)
    inverse(spec_x, spec_h, 1.0, 2)
    scatter(2)

    arrived(2)
    square = jnp.zeros((1, LANES), F32)
    cross = jnp.zeros((1, LANES), F32)
    for c in chunks:
        inner = recv[2, c, :] + gt[c, :] * send[1, c, :]
        gated = qt[c, :] * inner
        it[c, :] = inner
        ct[c, :] = gated
        square = square + jnp.sum(gated * gated, axis=0, keepdims=True)
        cross = cross + jnp.sum(st[c, :] * gated, axis=0, keepdims=True)
    norm_s[...] = jnp.zeros((8, LANES), F32)
    norm_s[0:1, :] = square
    norm_s[1:2, :] = cross
    pltpu.make_async_copy(norm_s, norm_r.at[lane], norm_recv).start()

    def share(i, carry):
        pltpu.make_async_remote_copy(
            src_ref=norm_s,
            dst_ref=norm_r.at[lane],
            send_sem=norm_send,
            recv_sem=norm_recv,
            device_id={"tensor": (lane + i) % n_ten},
            device_id_type=MESH,
        ).start()
        return carry

    lax.fori_loop(1, n_ten, share, 0)
    pltpu.make_async_copy(norm_r, norm_r, norm_recv).wait()
    total = norm_r[0]
    for i in range(1, 8):
        total = total + norm_r[i]
    scale = lax.rsqrt(total[0:1] / CHANNELS + EPS)
    pull = scale * scale * scale * (total[1:2] / CHANNELS)
    for c in chunks:
        d_gated = scale * st[c, :] - ct[c, :] * pull
        d_conv = d_gated * qt[c, :]
        send[3, c, :] = d_conv.astype(BF16).astype(F32)
        gt[c, :] = gt[c, :] * d_conv
        it[c, :] = d_gated * it[c, :]
    scatter(3)
    for c in chunks:
        out[:, c] = ((ct[c, :] * scale).T * gain[0:1, c]).astype(BF16)
        db[0, :, c] = it[c, :].T

    arrived(3)
    forward(3, spec_g)
    inverse(spec_g, spec_h, -1.0, 4)
    scatter(4)
    inverse(spec_g, spec_x, -1.0, 5)
    scatter(5)

    arrived(4)
    for c in chunks:
        d_mixed = recv[4, c, :] + gt[c, :]
        db[1, :, c] = (d_mixed * vt[c, :]).T
        db[2, :, c] = (d_mixed * kt[c, :]).T
    for i in range(3):
        halo_s[1, 2 * i : 2 * i + 2, :] = db[i, 0:2, :]
    halo_s[1, 6:8, :] = jnp.zeros((2, wide), F32)
    last_halo = halo_copy(1, (me + n_ctx - 1) % n_ctx)
    last_halo.start()
    last_halo.wait_recv()
    keep = (me < n_ctx - 1).astype(F32)
    for c in chunks:
        for i in range(3):
            x = db[i, :, c]
            near = halo_r[1, 2 * i : 2 * i + 1, c] * keep
            far = halo_r[1, 2 * i + 1 : 2 * i + 2, c] * keep
            x1 = jnp.where(row == LANES - 1, near, pltpu.roll(x, LANES - 1, 0))
            x2 = jnp.where(
                row == LANES - 1,
                far,
                jnp.where(row == LANES - 2, near, pltpu.roll(x, LANES - 2, 0)),
            )
            fgrad[i, :, c] = (
                taps[i, 0 : 1, c] * x
                + taps[i, 1 : 2, c] * x1
                + taps[i, 2 : 3, c] * x2
            )
    arrived(5)
    for c in chunks:
        hgrad[:, c] = recv[5, c, :].T

    for u in range(6):
        gone = pl.ds(0, (n_ctx - 1) * CH)
        pltpu.make_async_copy(send.at[u, gone], send.at[u, gone], send_sem.at[u]).wait()
    first_halo.wait_send()
    last_halo.wait_send()
    spent = pl.ds(0, n_ten - 1)
    pltpu.make_async_copy(norm_r.at[spent], norm_r.at[spent], norm_send).wait()


def deliver(a, b, c, a_out, b_out, c_out, a_mid, b_mid, c_mid, sem):
    mids = (a_mid, b_mid, c_mid)
    loads = [pltpu.make_async_copy(x, y, sem.at[i]) for i, (x, y) in enumerate(zip((a, b, c), mids))]
    stores = [
        pltpu.make_async_copy(x, y, sem.at[3 + i])
        for i, (x, y) in enumerate(zip(mids, (a_out, b_out, c_out)))
    ]
    for load in loads:
        load.start()
    for load, store in zip(loads, stores):
        load.wait()
        store.start()
    for store in stores:
        store.wait()


def per_device(features, short_filter, long_filter, skip_gain, norm_gain, out_grad):
    rows, wide = long_filter.shape
    anywhere = pl.BlockSpec(memory_space=pl.ANY)
    vmem = pl.BlockSpec(memory_space=pltpu.VMEM)
    column = pltpu.VMEM((wide, rows), F32)
    spec = pltpu.VMEM((wide, 2 * rows), F32)
    half = pltpu.VMEM((wide, 2 * rows), BF16)
    consts = jnp.asarray(constants(64, rows))
    operands = (
        features,
        short_filter,
        long_filter,
        skip_gain.reshape(1, wide),
        norm_gain.reshape(1, wide),
        out_grad,
        consts,
    )
    shapes = (
        jax.ShapeDtypeStruct((rows, wide), BF16),
        jax.ShapeDtypeStruct((3, rows, wide), F32),
        jax.ShapeDtypeStruct((rows, wide), F32),
    )
    results = pl.pallas_call(
        kernel,
        out_shape=shapes,
        in_specs=[anywhere] * N_IN,
        out_specs=[vmem] * 3,
        scratch_shapes=[
            pltpu.VMEM((6, wide, rows), F32),
            pltpu.VMEM((6, wide, rows), F32),
        ]
        + [column] * 7
        + [spec] * 3
        + [half] * 2
        + [
            pltpu.VMEM((3, rows, wide), F32),
            pltpu.VMEM((2, 8, wide), F32),
            pltpu.VMEM((2, 8, wide), F32),
            pltpu.VMEM((8, rows), F32),
            pltpu.VMEM((8, 8, rows), F32),
            pltpu.VMEM((256, 64), BF16),
            pltpu.VMEM((256, 256), BF16),
            pltpu.VMEM((256, 256), BF16),
            pltpu.VMEM((64, 128), BF16),
            pltpu.VMEM((64, 128), BF16),
            pltpu.VMEM((256, 256), BF16),
            pltpu.VMEM((256, 256), BF16),
            pltpu.VMEM((64, 128), F32),
            pltpu.VMEM((64, 128), F32),
            pltpu.SemaphoreType.DMA((6,)),
            pltpu.SemaphoreType.DMA((6,)),
            pltpu.SemaphoreType.DMA((2,)),
            pltpu.SemaphoreType.DMA((2,)),
            pltpu.SemaphoreType.DMA,
            pltpu.SemaphoreType.DMA,
            pltpu.SemaphoreType.DMA((N_IN,)),
        ]
        + [pltpu.VMEM(x.shape, x.dtype) for x in operands],
        compiler_params=pltpu.CompilerParams(
            collective_id=0, has_side_effects=True, vmem_limit_bytes=VMEM_BYTES
        ),
    )(*operands)
    return pl.pallas_call(
        deliver,
        out_shape=shapes,
        in_specs=[anywhere] * 3,
        out_specs=[anywhere] * 3,
        scratch_shapes=[pltpu.VMEM(x.shape, x.dtype) for x in shapes]
        + [pltpu.SemaphoreType.DMA((6,))],
        compiler_params=pltpu.CompilerParams(vmem_limit_bytes=VMEM_BYTES),
    )(*results)


def solution(mesh):
    return jax.shard_map(
        per_device,
        mesh=mesh,
        in_specs=(
            P(None, "context", "tensor"),
            P(None, None, "tensor"),
            P("context", "tensor"),
            P("tensor"),
            P("tensor"),
            P("context", "tensor"),
        ),
        out_specs=(P("context", "tensor"), P(None, "context", "tensor"), P("context", "tensor")),
        check_vma=False,
    )
```

```python
import functools

import jax
import jax.numpy as jnp
import numpy as np
from jax import lax
from jax.experimental import pallas as pl
from jax.experimental.pallas import tpu as pltpu
from jax.sharding import PartitionSpec as P

CHANNELS = 4096
EPS = 1e-06
F32 = jnp.float32
BF16 = jnp.bfloat16
MESH = pl.DeviceIdType.MESH
RING = 16
SIDE = 4
LANES = 128
CH = 8
HALF = CH // 2
N_IN = 7
VMEM_BYTES = 63 * 1024 * 1024


def constants(blocks, width):
    length = 2 * blocks * width
    a = np.arange(blocks)
    k1 = np.arange(blocks) + 0.5
    first = 2.0 * np.pi * k1[:, None] * a[None, :] / (2 * blocks)
    f1 = np.concatenate([np.cos(first), -np.sin(first)], axis=0)
    g1 = np.concatenate([np.cos(first.T), -np.sin(first.T)], axis=1) * (2.0 / length)
    b = np.arange(width)
    twist = 2.0 * np.pi * k1[:, None] * b[None, :] / length
    second = 2.0 * np.pi * ((b[:, None] * b[None, :]) % width) / width
    c, s = np.cos(second), np.sin(second)
    f2 = np.block([[c, -s], [s, c]])
    g2 = np.block([[c, s], [-s, c]])

    pack = np.zeros((6 * width, 2 * width), np.float32)
    pack[: 2 * width] = f2
    pack[2 * width : 4 * width] = g2
    pack[4 * width : 5 * width, :blocks] = f1
    pack[5 * width : 5 * width + blocks, :width] = g1
    pack[5 * width + blocks : 6 * width, :width] = np.cos(twist)
    pack[5 * width + blocks : 6 * width, width:] = np.sin(twist)
    return pack


def dot(a, b):
    return jnp.dot(a, b, preferred_element_type=F32)


def halves(x):
    high = x.astype(BF16)
    return high, (x - high.astype(F32)).astype(BF16)


def kernel(
    *refs,
):
    held, (out, fgrad, hgrad) = refs[:N_IN], refs[N_IN : N_IN + 3]
    (send, recv, qt, kt, vt, st, it, gt, ct, spec_h, spec_x, spec_g, th, tl, db,
     halo_s, halo_r, norm_s, norm_r,
     f1, f2h, f2l, g1h, g1l, g2h, g2l, wr, wi,
     send_sem, recv_sem, halo_send, halo_recv, norm_send, norm_recv, in_sem, ring_sem,
     out_v, fgrad_v, out_sem) = refs[N_IN + 3 : -N_IN]
    local = refs[-N_IN:]
    feat, taps, filt, skip, gain, grad, consts = local
    fetch = [
        pltpu.make_async_copy(held[i], local[i], in_sem.at[i]) for i in range(N_IN)
    ]
    early = (2, 0)
    late = [i for i in range(N_IN) if i not in early]
    for i in early:
        fetch[i].start()
    me = lax.axis_index("context")
    lane = lax.axis_index("tensor")
    n_ctx = lax.axis_size("context")
    n_ten = lax.axis_size("tensor")
    my_z, my_y = me // SIDE, me % SIDE
    wide = LANES * SIDE
    chunks = [slice(j * LANES, (j + 1) * LANES) for j in range(wide // LANES)]

    def peer(i):
        i = n_ctx - i
        k = i // SIDE
        odd = k % 2
        dz = odd * ((k + 1) // 2) + (1 - odd) * (RING - k // 2)
        return ((my_z + dz) % RING) * SIDE + (my_y + i % SIDE) % SIDE

    barrier = pltpu.get_barrier_semaphore()

    def greet_z(i, carry):
        p = ((my_z + i) % RING) * SIDE + my_y
        pl.semaphore_signal(barrier, inc=1, device_id={"context": p}, device_id_type=MESH)
        return carry

    def greet_tensor(i, carry):
        pl.semaphore_signal(
            barrier, inc=1, device_id={"tensor": (lane + i) % n_ten}, device_id_type=MESH
        )
        return carry

    beside = [my_z * SIDE + (my_y + i) % SIDE for i in range(1, SIDE)]
    lax.fori_loop(1, RING, greet_z, 0)
    for p in beside:
        pl.semaphore_signal(barrier, inc=1, device_id={"context": p}, device_id_type=MESH)
    lax.fori_loop(1, n_ten, greet_tensor, 0)
    for i in late:
        fetch[i].start()

    def piece(i, part):
        if part is None:
            return pl.ds(pl.multiple_of(i * CH, CH), CH)
        return pl.ds(pl.multiple_of(i * CH + part * HALF, HALF), HALF)

    def scatter(u, part=None, land=None, even_first=False):
        slot = 2 * u + (part or 0)
        land = recv.at[u] if land is None else land
        mine = piece(me, part)
        pltpu.make_async_copy(send.at[u, mine], land.at[mine], recv_sem.at[slot]).start()

        def push(p):
            pltpu.make_async_remote_copy(
                src_ref=send.at[u, piece(p, part)],
                dst_ref=land.at[mine],
                send_sem=send_sem.at[u],
                recv_sem=recv_sem.at[slot],
                device_id={"context": p},
                device_id_type=MESH,
            ).start()

        def body(i, carry):
            push(peer(i))
            return carry

        if not even_first:
            lax.fori_loop(1, n_ctx, body, 0)
            return
        same = my_z % 2
        for odd, count in ((same, 31 + same), (1 - same, 32 - same)):

            def by_parity(i, carry, odd=odd):
                j = i // SIDE
                dz = (8 - odd - 2 * ((j + 1 - odd) // 2)) * (2 * ((j + odd) % 2) - 1)
                push(((my_z + dz + RING) % RING) * SIDE + (my_y + i + 1) % SIDE)
                return carry

            lax.fori_loop(0, count, by_parity, 0)

    def arrived(u, part=None, land=None):
        slot = 2 * u + (part or 0)
        land = recv.at[u] if land is None else land
        size = pl.ds(0, n_ctx * (CH if part is None else HALF))
        pltpu.make_async_copy(send.at[u, size], land.at[size], recv_sem.at[slot]).wait()

    def halo_copy(h, to):
        return pltpu.make_async_remote_copy(
            src_ref=halo_s.at[h],
            dst_ref=halo_r.at[h],
            send_sem=halo_send.at[h],
            recv_sem=halo_recv.at[h],
            device_id={"context": to},
            device_id_type=MESH,
        )

    fetch[2].wait()
    for j, c in enumerate(chunks):
        send[0, c, :] = filt[:, c].astype(F32).T
    fetch[0].wait()
    for i in range(3):
        halo_s[0, 2 * i : 2 * i + 2, :] = feat[i, 112:128, :].astype(F32)[14:16]
    halo_s[0, 6:8, :] = jnp.zeros((2, wide), F32)
    pl.semaphore_wait(barrier, RING - 1 + SIDE - 1 + n_ten - 1)
    for p in beside:
        pl.semaphore_signal(ring_sem, inc=1, device_id={"context": p}, device_id_type=MESH)
    pl.semaphore_wait(ring_sem, SIDE - 1)

    first_halo = halo_copy(0, (me + 1) % n_ctx)
    first_halo.start()
    scatter(0)
    for i in late:
        fetch[i].wait()
    f2h[...], f2l[...] = halves(consts[0:256, :])
    g2h[...], g2l[...] = halves(consts[256:512, :])
    f1[0:128, :], f1[128:256, :] = halves(consts[512:640, 0:64])
    g1h[...], g1l[...] = halves(consts[640:704, 0:128])
    wr[...] = consts[704:768, 0:128]
    wi[...] = consts[704:768, 128:256]

    for j, c in enumerate(chunks):
        st[c, :] = (grad[:, c].astype(F32) * gain[0:1, c]).T
        gt[c, :] = jnp.broadcast_to(skip[0:1, c], (LANES, LANES)).T

    row = lax.broadcasted_iota(jnp.int32, (LANES, LANES), 0)
    first_halo.wait_recv()
    keep = (me > 0).astype(F32)
    for j, c in enumerate(chunks):
        parts = []
        for i in range(3):
            x = feat[i, :, c].astype(F32)
            far = halo_r[0, 2 * i : 2 * i + 1, c] * keep
            near = halo_r[0, 2 * i + 1 : 2 * i + 2, c] * keep
            x1 = jnp.where(row == 0, near, pltpu.roll(x, 1, 0))
            x2 = jnp.where(row == 0, far, jnp.where(row == 1, near, pltpu.roll(x, 2, 0)))
            parts.append(
                taps[i, 0 : 1, c] * x
                + taps[i, 1 : 2, c] * x1
                + taps[i, 2 : 3, c] * x2
            )
        qt[c, :] = parts[0].T
        k, v = parts[1].T, parts[2].T
        kt[c, :] = k
        vt[c, :] = v
        send[1, c, :] = (k * v).astype(BF16).astype(F32)
    scatter(1, 0)
    scatter(1, 1)

    blocks = 64

    def forward(u, spec, part):
        for p in range(part * HALF // 2, (part + 1) * HALF // 2):
            x = jnp.concatenate(
                [recv[u, pl.ds(2 * p + e, blocks, stride=CH), :] for e in range(2)], axis=1
            ).astype(BF16)
            z = dot(f1[...], x)
            z = z[: 2 * blocks] + z[2 * blocks :]
            for e in range(2):
                re = z[:blocks, e * LANES : (e + 1) * LANES]
                im = z[blocks:, e * LANES : (e + 1) * LANES]
                rows = slice((2 * p + e) * blocks, (2 * p + e + 1) * blocks)
                h, l = halves(re * wr[...] + im * wi[...])
                th[rows, :LANES] = h
                tl[rows, :LANES] = l
                h, l = halves(im * wr[...] - re * wi[...])
                th[rows, LANES:] = h
                tl[rows, LANES:] = l
        rows = slice(part * HALF * blocks, (part + 1) * HALF * blocks)
        spec[rows, :] = dot(th[rows, :], f2h[...]) + dot(tl[rows, :], f2h[...]) + dot(th[rows, :], f2l[...])

    def inverse(a, b, sign, u, part):
        for p in range(part * HALF // 2, (part + 1) * HALF // 2):
            rows = slice(2 * p * blocks, 2 * (p + 1) * blocks)
            ar, ai = a[rows, :LANES], a[rows, LANES:]
            br, bi = b[rows, :LANES], sign * b[rows, LANES:]
            h, l = halves(ar * br - ai * bi)
            th[rows, :LANES] = h
            tl[rows, :LANES] = l
            h, l = halves(ar * bi + ai * br)
            th[rows, LANES:] = h
            tl[rows, LANES:] = l
        base = part * HALF * blocks
        rows = slice(base, base + HALF * blocks)
        t = dot(th[rows, :], g2h[...]) + dot(tl[rows, :], g2h[...]) + dot(th[rows, :], g2l[...])
        for p in range(part * HALF // 2, (part + 1) * HALF // 2):
            both = []
            for e in range(2):
                rows = slice((2 * p + e) * blocks - base, (2 * p + e + 1) * blocks - base)
                re, im = t[rows, :LANES], t[rows, LANES:]
                both.append(
                    jnp.concatenate(
                        [re * wr[...] - im * wi[...], im * wr[...] + re * wi[...]], axis=0
                    )
                )
            h, l = halves(jnp.concatenate(both, axis=1))
            y = dot(g1h[...], h) + dot(g1h[...], l) + dot(g1l[...], h)
            for e in range(2):
                send[u, pl.ds(2 * p + e, blocks, stride=CH), :] = y[:, e * LANES : (e + 1) * LANES]

    arrived(0)
    for part in range(2):
        forward(0, spec_h, part)
    for part in range(2):
        arrived(1, part)
        forward(1, spec_x, part)
        inverse(spec_x, spec_h, 1.0, 2, part)
        scatter(2, part, even_first=True)

    for part in range(2):
        arrived(2, part)
    square = jnp.zeros((1, LANES), F32)
    cross = jnp.zeros((1, LANES), F32)
    for c in chunks:
        inner = recv[2, c, :] + gt[c, :] * send[1, c, :]
        gated = qt[c, :] * inner
        it[c, :] = inner
        ct[c, :] = gated
        square = square + jnp.sum(gated * gated, axis=0, keepdims=True)
        cross = cross + jnp.sum(st[c, :] * gated, axis=0, keepdims=True)
    norm_s[...] = jnp.zeros((8, LANES), F32)
    norm_s[0:1, :] = square
    norm_s[1:2, :] = cross
    pltpu.make_async_copy(norm_s, norm_r.at[lane], norm_recv).start()

    def share(i, carry):
        pltpu.make_async_remote_copy(
            src_ref=norm_s,
            dst_ref=norm_r.at[lane],
            send_sem=norm_send,
            recv_sem=norm_recv,
            device_id={"tensor": (lane + i) % n_ten},
            device_id_type=MESH,
        ).start()
        return carry

    lax.fori_loop(1, n_ten, share, 0)
    pltpu.make_async_copy(norm_r, norm_r, norm_recv).wait()
    total = norm_r[0]
    for i in range(1, 8):
        total = total + norm_r[i]
    scale = lax.rsqrt(total[0:1] / CHANNELS + EPS)
    pull = scale * scale * scale * (total[1:2] / CHANNELS)
    for c in chunks:
        d_gated = scale * st[c, :] - ct[c, :] * pull
        d_conv = d_gated * qt[c, :]
        send[3, c, :] = d_conv.astype(BF16).astype(F32)
        gt[c, :] = gt[c, :] * d_conv
        it[c, :] = d_gated * it[c, :]
    scatter(3, 0)
    scatter(3, 1)
    for c in chunks:
        out_v[:, c] = ((ct[c, :] * scale).T * gain[0:1, c]).astype(BF16)
        db[0, :, c] = it[c, :].T

    out_copy = pltpu.make_async_copy(out_v, out, out_sem.at[0])
    out_copy.start()
    for part in range(2):
        arrived(3, part)
        forward(3, spec_g, part)
        inverse(spec_g, spec_h, -1.0, 4, part)
        scatter(4, part)
        inverse(spec_g, spec_x, -1.0, 5, part)
    scatter(5, land=hgrad)
    for part in range(2):
        arrived(4, part)
    for c in chunks:
        d_mixed = recv[4, c, :] + gt[c, :]
        db[1, :, c] = (d_mixed * vt[c, :]).T
        db[2, :, c] = (d_mixed * kt[c, :]).T
    for i in range(3):
        halo_s[1, 2 * i : 2 * i + 2, :] = db[i, 0:2, :]
    halo_s[1, 6:8, :] = jnp.zeros((2, wide), F32)
    last_halo = halo_copy(1, (me + n_ctx - 1) % n_ctx)
    last_halo.start()
    last_halo.wait_recv()
    keep = (me < n_ctx - 1).astype(F32)
    for c in chunks:
        for i in range(3):
            x = db[i, :, c]
            near = halo_r[1, 2 * i : 2 * i + 1, c] * keep
            far = halo_r[1, 2 * i + 1 : 2 * i + 2, c] * keep
            x1 = jnp.where(row == LANES - 1, near, pltpu.roll(x, LANES - 1, 0))
            x2 = jnp.where(
                row == LANES - 1,
                far,
                jnp.where(row == LANES - 2, near, pltpu.roll(x, LANES - 2, 0)),
            )
            fgrad_v[i, :, c] = (
                taps[i, 0 : 1, c] * x
                + taps[i, 1 : 2, c] * x1
                + taps[i, 2 : 3, c] * x2
            )
    fgrad_copy = pltpu.make_async_copy(fgrad_v, fgrad, out_sem.at[1])
    fgrad_copy.start()
    arrived(5, land=hgrad)
    out_copy.wait()
    fgrad_copy.wait()

    for u in range(6):
        gone = pl.ds(0, (n_ctx - 1) * CH)
        pltpu.make_async_copy(send.at[u, gone], send.at[u, gone], send_sem.at[u]).wait()
    first_halo.wait_send()
    last_halo.wait_send()
    spent = pl.ds(0, n_ten - 1)
    pltpu.make_async_copy(norm_r.at[spent], norm_r.at[spent], norm_send).wait()


def deliver(a, b, c, a_out, b_out, c_out, a_mid, b_mid, c_mid, c_turned, sem):
    loads = [
        pltpu.make_async_copy(x, y, sem.at[i])
        for i, (x, y) in enumerate(((c, c_mid), (b, b_mid), (a, a_mid)))
    ]
    stores = [
        pltpu.make_async_copy(x, y, sem.at[3 + i])
        for i, (x, y) in enumerate(((c_turned, c_out), (b_mid, b_out), (a_mid, a_out)))
    ]
    for load in loads:
        load.start()
    for load, store in zip(loads, stores):
        load.wait()
        if load is loads[0]:
            for j in range(0, c_mid.shape[0], LANES):
                c_turned[:, j : j + LANES] = c_mid[j : j + LANES, :].T
        store.start()
    for store in stores:
        store.wait()


def per_device(features, short_filter, long_filter, skip_gain, norm_gain, out_grad):
    rows, wide = long_filter.shape
    anywhere = pl.BlockSpec(memory_space=pl.ANY)
    column = pltpu.VMEM((wide, rows), F32)
    spec = pltpu.VMEM((wide, 2 * rows), F32)
    half = pltpu.VMEM((wide, 2 * rows), BF16)
    consts = jnp.asarray(constants(64, rows))
    operands = (
        features,
        short_filter,
        long_filter,
        skip_gain.reshape(1, wide),
        norm_gain.reshape(1, wide),
        out_grad,
        consts,
    )
    shapes = (
        jax.ShapeDtypeStruct((rows, wide), BF16),
        jax.ShapeDtypeStruct((3, rows, wide), F32),
        jax.ShapeDtypeStruct((rows, wide), F32),
    )
    column_grad = jax.ShapeDtypeStruct((wide, rows), F32)
    results = pl.pallas_call(
        kernel,
        out_shape=shapes[:2] + (column_grad,),
        in_specs=[anywhere] * N_IN,
        out_specs=[anywhere] * 3,
        scratch_shapes=[
            pltpu.VMEM((6, wide, rows), F32),
            pltpu.VMEM((6, wide, rows), F32),
        ]
        + [column] * 7
        + [spec] * 3
        + [half] * 2
        + [
            pltpu.VMEM((3, rows, wide), F32),
            pltpu.VMEM((2, 8, wide), F32),
            pltpu.VMEM((2, 8, wide), F32),
            pltpu.VMEM((8, rows), F32),
            pltpu.VMEM((8, 8, rows), F32),
            pltpu.VMEM((256, 64), BF16),
            pltpu.VMEM((256, 256), BF16),
            pltpu.VMEM((256, 256), BF16),
            pltpu.VMEM((64, 128), BF16),
            pltpu.VMEM((64, 128), BF16),
            pltpu.VMEM((256, 256), BF16),
            pltpu.VMEM((256, 256), BF16),
            pltpu.VMEM((64, 128), F32),
            pltpu.VMEM((64, 128), F32),
            pltpu.SemaphoreType.DMA((6,)),
            pltpu.SemaphoreType.DMA((12,)),
            pltpu.SemaphoreType.DMA((2,)),
            pltpu.SemaphoreType.DMA((2,)),
            pltpu.SemaphoreType.DMA,
            pltpu.SemaphoreType.DMA,
            pltpu.SemaphoreType.DMA((N_IN,)),
            pltpu.SemaphoreType.REGULAR,
            pltpu.VMEM((rows, wide), BF16),
            pltpu.VMEM((3, rows, wide), F32),
            pltpu.SemaphoreType.DMA((2,)),
        ]
        + [pltpu.VMEM(x.shape, x.dtype) for x in operands],
        compiler_params=pltpu.CompilerParams(
            collective_id=0, has_side_effects=True, vmem_limit_bytes=VMEM_BYTES
        ),
    )(*operands)
    return pl.pallas_call(
        deliver,
        out_shape=shapes,
        in_specs=[anywhere] * 3,
        out_specs=[anywhere] * 3,
        scratch_shapes=[pltpu.VMEM(x.shape, x.dtype) for x in shapes[:2] + (column_grad, shapes[2])]
        + [pltpu.SemaphoreType.DMA((6,))],
        compiler_params=pltpu.CompilerParams(vmem_limit_bytes=VMEM_BYTES),
    )(*results)


def solution(mesh):
    return jax.shard_map(
        per_device,
        mesh=mesh,
        in_specs=(
            P(None, "context", "tensor"),
            P(None, None, "tensor"),
            P("context", "tensor"),
            P("tensor"),
            P("tensor"),
            P("context", "tensor"),
        ),
        out_specs=(P("context", "tensor"), P(None, "context", "tensor"), P("context", "tensor")),
        check_vma=False,
    )
```

```python
import functools

import jax
import jax.numpy as jnp
import numpy as np
from jax import lax
from jax.experimental import pallas as pl
from jax.experimental.pallas import tpu as pltpu
from jax.sharding import PartitionSpec as P

CHANNELS = 4096
EPS = 1e-06
F32 = jnp.float32
BF16 = jnp.bfloat16
MESH = pl.DeviceIdType.MESH
RING = 16
SIDE = 4
LANES = 128
CH = 8
HALF = CH // 2
N_IN = 7
VMEM_BYTES = 63 * 1024 * 1024


def constants(blocks, width):
    length = 2 * blocks * width
    a = np.arange(blocks)
    k1 = np.arange(blocks) + 0.5
    first = 2.0 * np.pi * k1[:, None] * a[None, :] / (2 * blocks)
    f1 = np.concatenate([np.cos(first), -np.sin(first)], axis=0)
    g1 = np.concatenate([np.cos(first.T), -np.sin(first.T)], axis=1) * (2.0 / length)
    b = np.arange(width)
    twist = 2.0 * np.pi * k1[:, None] * b[None, :] / length
    second = 2.0 * np.pi * ((b[:, None] * b[None, :]) % width) / width
    c, s = np.cos(second), np.sin(second)
    f2 = np.block([[c, -s], [s, c]])
    g2 = np.block([[c, s], [-s, c]])

    pack = np.zeros((6 * width, 2 * width), np.float32)
    pack[: 2 * width] = f2
    pack[2 * width : 4 * width] = g2
    pack[4 * width : 5 * width, :blocks] = f1
    pack[5 * width : 5 * width + blocks, :width] = g1
    pack[5 * width + blocks : 6 * width, :width] = np.cos(twist)
    pack[5 * width + blocks : 6 * width, width:] = np.sin(twist)
    return pack


def dot(a, b):
    return jnp.dot(a, b, preferred_element_type=F32)


def halves(x):
    high = x.astype(BF16)
    return high, (x - high.astype(F32)).astype(BF16)


def kernel(
    *refs,
):
    held, (out, fgrad, hgrad) = refs[:N_IN], refs[N_IN : N_IN + 3]
    (send, recv, qt, kt, vt, st, it, gt, ct, spec_h, spec_x, spec_g, th, tl, db,
     halo_s, halo_r, norm_s, norm_r,
     f1, f2h, f2l, g1h, g1l, g2h, g2l, wr, wi,
     send_sem, recv_sem, halo_send, halo_recv, norm_send, norm_recv, in_sem, ring_sem,
     out_v, fgrad_v, out_sem) = refs[N_IN + 3 : -N_IN]
    local = refs[-N_IN:]
    feat, taps, filt, skip, gain, grad, consts = local
    fetch = [
        pltpu.make_async_copy(held[i], local[i], in_sem.at[i]) for i in range(N_IN)
    ]
    early = (2, 0)
    late = [i for i in range(N_IN) if i not in early]
    for i in early:
        fetch[i].start()
    me = lax.axis_index("context")
    lane = lax.axis_index("tensor")
    n_ctx = lax.axis_size("context")
    n_ten = lax.axis_size("tensor")
    my_z, my_y = me // SIDE, me % SIDE
    wide = LANES * SIDE
    chunks = [slice(j * LANES, (j + 1) * LANES) for j in range(wide // LANES)]

    columns = [(my_y + i) % SIDE for i in (2, 1, 3, 0)]

    def ring_row(j):
        k = RING - 1 - j
        odd = (k + lane) % 2
        m = k // 2 + k % 2
        dz = odd * m + (1 - odd) * (RING - m)
        return ((my_z + dz) % RING) * SIDE

    barrier = pltpu.get_barrier_semaphore()

    def greet_z(i, carry):
        p = ((my_z + i) % RING) * SIDE + my_y
        pl.semaphore_signal(barrier, inc=1, device_id={"context": p}, device_id_type=MESH)
        return carry

    def greet_tensor(i, carry):
        pl.semaphore_signal(
            barrier, inc=1, device_id={"tensor": (lane + i) % n_ten}, device_id_type=MESH
        )
        return carry

    beside = [my_z * SIDE + (my_y + i) % SIDE for i in range(1, SIDE)]
    lax.fori_loop(1, RING, greet_z, 0)
    for p in beside:
        pl.semaphore_signal(barrier, inc=1, device_id={"context": p}, device_id_type=MESH)
    lax.fori_loop(1, n_ten, greet_tensor, 0)
    for i in late:
        fetch[i].start()

    def piece(i, part):
        if part is None:
            return pl.ds(pl.multiple_of(i * CH, CH), CH)
        return pl.ds(pl.multiple_of(i * CH + part * HALF, HALF), HALF)

    def scatter(u, part=None, land=None, first=0):
        slot = 2 * u + (part or 0)
        land = recv.at[u] if land is None else land
        mine = piece(me, part)
        pltpu.make_async_copy(send.at[u, mine], land.at[mine], recv_sem.at[slot]).start()

        def push(p):
            pltpu.make_async_remote_copy(
                src_ref=send.at[u, piece(p, part)],
                dst_ref=land.at[mine],
                send_sem=send_sem.at[u],
                recv_sem=recv_sem.at[slot],
                device_id={"context": p},
                device_id_type=MESH,
            ).start()

        def body(j, carry):
            row = ring_row(j)
            if first:

                @pl.when(row >= first * SIDE)
                def _():
                    for y in columns:
                        push(row + y)

            else:
                for y in columns:
                    push(row + y)
            return carry

        def ahead(i, carry):
            row = ((i + my_z) % first) * SIDE
            for y in columns:

                @pl.when(row + y != me)
                def _():
                    push(row + y)

            return carry

        def own_row():
            for y in columns[:-1]:
                push(my_z * SIDE + y)

        if first:
            lax.fori_loop(0, first, ahead, 0)
        lax.fori_loop(0, RING - 1, body, 0)
        if first:
            pl.when(my_z >= first)(own_row)
        else:
            own_row()

    def arrived(u, part=None, land=None):
        slot = 2 * u + (part or 0)
        land = recv.at[u] if land is None else land
        size = pl.ds(0, n_ctx * (CH if part is None else HALF))
        pltpu.make_async_copy(send.at[u, size], land.at[size], recv_sem.at[slot]).wait()

    def halo_copy(h, to):
        return pltpu.make_async_remote_copy(
            src_ref=halo_s.at[h],
            dst_ref=halo_r.at[h],
            send_sem=halo_send.at[h],
            recv_sem=halo_recv.at[h],
            device_id={"context": to},
            device_id_type=MESH,
        )

    fetch[2].wait()
    for j, c in enumerate(chunks):
        send[0, c, :] = filt[:, c].astype(F32).T
    fetch[0].wait()
    for i in range(3):
        halo_s[0, 2 * i : 2 * i + 2, :] = feat[i, 112:128, :].astype(F32)[14:16]
    halo_s[0, 6:8, :] = jnp.zeros((2, wide), F32)
    pl.semaphore_wait(barrier, RING - 1 + SIDE - 1 + n_ten - 1)
    for p in beside:
        pl.semaphore_signal(ring_sem, inc=1, device_id={"context": p}, device_id_type=MESH)
    pl.semaphore_wait(ring_sem, SIDE - 1)

    first_halo = halo_copy(0, (me + 1) % n_ctx)
    first_halo.start()
    scatter(0)
    for i in late:
        fetch[i].wait()
    f2h[...], f2l[...] = halves(consts[0:256, :])
    g2h[...], g2l[...] = halves(consts[256:512, :])
    f1[0:128, :], f1[128:256, :] = halves(consts[512:640, 0:64])
    g1h[...], g1l[...] = halves(consts[640:704, 0:128])
    wr[...] = consts[704:768, 0:128]
    wi[...] = consts[704:768, 128:256]

    for j, c in enumerate(chunks):
        st[c, :] = (grad[:, c].astype(F32) * gain[0:1, c]).T
        gt[c, :] = jnp.broadcast_to(skip[0:1, c], (LANES, LANES)).T

    row = lax.broadcasted_iota(jnp.int32, (LANES, LANES), 0)
    first_halo.wait_recv()
    keep = (me > 0).astype(F32)
    for j, c in enumerate(chunks):
        parts = []
        for i in range(3):
            x = feat[i, :, c].astype(F32)
            far = halo_r[0, 2 * i : 2 * i + 1, c] * keep
            near = halo_r[0, 2 * i + 1 : 2 * i + 2, c] * keep
            x1 = jnp.where(row == 0, near, pltpu.roll(x, 1, 0))
            x2 = jnp.where(row == 0, far, jnp.where(row == 1, near, pltpu.roll(x, 2, 0)))
            parts.append(
                taps[i, 0 : 1, c] * x
                + taps[i, 1 : 2, c] * x1
                + taps[i, 2 : 3, c] * x2
            )
        qt[c, :] = parts[0].T
        k, v = parts[1].T, parts[2].T
        kt[c, :] = k
        vt[c, :] = v
        send[1, c, :] = (k * v).astype(BF16).astype(F32)
    scatter(1, 0)
    scatter(1, 1)

    blocks = 64

    def forward(u, spec, part):
        for p in range(part * HALF // 2, (part + 1) * HALF // 2):
            x = jnp.concatenate(
                [recv[u, pl.ds(2 * p + e, blocks, stride=CH), :] for e in range(2)], axis=1
            ).astype(BF16)
            z = dot(f1[...], x)
            z = z[: 2 * blocks] + z[2 * blocks :]
            for e in range(2):
                re = z[:blocks, e * LANES : (e + 1) * LANES]
                im = z[blocks:, e * LANES : (e + 1) * LANES]
                rows = slice((2 * p + e) * blocks, (2 * p + e + 1) * blocks)
                h, l = halves(re * wr[...] + im * wi[...])
                th[rows, :LANES] = h
                tl[rows, :LANES] = l
                h, l = halves(im * wr[...] - re * wi[...])
                th[rows, LANES:] = h
                tl[rows, LANES:] = l
        rows = slice(part * HALF * blocks, (part + 1) * HALF * blocks)
        spec[rows, :] = dot(th[rows, :], f2h[...]) + dot(tl[rows, :], f2h[...]) + dot(th[rows, :], f2l[...])

    def inverse(a, b, sign, u, part):
        for p in range(part * HALF // 2, (part + 1) * HALF // 2):
            rows = slice(2 * p * blocks, 2 * (p + 1) * blocks)
            ar, ai = a[rows, :LANES], a[rows, LANES:]
            br, bi = b[rows, :LANES], sign * b[rows, LANES:]
            h, l = halves(ar * br - ai * bi)
            th[rows, :LANES] = h
            tl[rows, :LANES] = l
            h, l = halves(ar * bi + ai * br)
            th[rows, LANES:] = h
            tl[rows, LANES:] = l
        base = part * HALF * blocks
        rows = slice(base, base + HALF * blocks)
        t = dot(th[rows, :], g2h[...]) + dot(tl[rows, :], g2h[...]) + dot(th[rows, :], g2l[...])
        for p in range(part * HALF // 2, (part + 1) * HALF // 2):
            both = []
            for e in range(2):
                rows = slice((2 * p + e) * blocks - base, (2 * p + e + 1) * blocks - base)
                re, im = t[rows, :LANES], t[rows, LANES:]
                both.append(
                    jnp.concatenate(
                        [re * wr[...] - im * wi[...], im * wr[...] + re * wi[...]], axis=0
                    )
                )
            h, l = halves(jnp.concatenate(both, axis=1))
            y = dot(g1h[...], h) + dot(g1h[...], l) + dot(g1l[...], h)
            for e in range(2):
                send[u, pl.ds(2 * p + e, blocks, stride=CH), :] = y[:, e * LANES : (e + 1) * LANES]

    arrived(0)
    for part in range(2):
        forward(0, spec_h, part)
    for part in range(2):
        arrived(1, part)
        forward(1, spec_x, part)
        inverse(spec_x, spec_h, 1.0, 2, part)
        scatter(2, part)

    for part in range(2):
        arrived(2, part)
    square = jnp.zeros((1, LANES), F32)
    cross = jnp.zeros((1, LANES), F32)
    for c in chunks:
        inner = recv[2, c, :] + gt[c, :] * send[1, c, :]
        gated = qt[c, :] * inner
        it[c, :] = inner
        ct[c, :] = gated
        square = square + jnp.sum(gated * gated, axis=0, keepdims=True)
        cross = cross + jnp.sum(st[c, :] * gated, axis=0, keepdims=True)
    norm_s[0:1, :] = square
    norm_s[1:2, :] = cross
    pltpu.make_async_copy(norm_s, norm_r.at[lane], norm_recv).start()

    def share(i, carry):
        pltpu.make_async_remote_copy(
            src_ref=norm_s,
            dst_ref=norm_r.at[lane],
            send_sem=norm_send,
            recv_sem=norm_recv,
            device_id={"tensor": (lane + i) % n_ten},
            device_id_type=MESH,
        ).start()
        return carry

    lax.fori_loop(1, n_ten, share, 0)
    pltpu.make_async_copy(norm_r, norm_r, norm_recv).wait()
    total = norm_r[0]
    for i in range(1, 8):
        total = total + norm_r[i]
    scale = lax.rsqrt(total[0:1] / CHANNELS + EPS)
    pull = scale * scale * scale * (total[1:2] / CHANNELS)
    for c in chunks:
        d_gated = scale * st[c, :] - ct[c, :] * pull
        send[3, c, :] = (d_gated * qt[c, :]).astype(BF16).astype(F32)
    scatter(3, 0)
    scatter(3, 1)
    for c in chunks:
        d_gated = scale * st[c, :] - ct[c, :] * pull
        gt[c, :] = gt[c, :] * (d_gated * qt[c, :])
        it[c, :] = d_gated * it[c, :]
    for c in chunks:
        out_v[:, c] = ((ct[c, :] * scale).T * gain[0:1, c]).astype(BF16)
        db[0, :, c] = it[c, :].T

    out_copy = pltpu.make_async_copy(out_v, out, out_sem.at[0])
    out_copy.start()
    for part in range(2):
        arrived(3, part)
        forward(3, spec_g, part)
        inverse(spec_g, spec_h, -1.0, 4, part)
        scatter(4, part)
        inverse(spec_g, spec_x, -1.0, 5, part)
    scatter(5, land=hgrad, first=4)
    for part in range(2):
        arrived(4, part)
    for c in chunks:
        d_mixed = recv[4, c, :] + gt[c, :]
        db[1, :, c] = (d_mixed * vt[c, :]).T
        db[2, :, c] = (d_mixed * kt[c, :]).T
    for i in range(3):
        halo_s[1, 2 * i : 2 * i + 2, :] = db[i, 0:2, :]
    halo_s[1, 6:8, :] = jnp.zeros((2, wide), F32)
    last_halo = halo_copy(1, (me + n_ctx - 1) % n_ctx)
    last_halo.start()
    last_halo.wait_recv()
    keep = (me < n_ctx - 1).astype(F32)
    for c in chunks:
        for i in range(3):
            x = db[i, :, c]
            near = halo_r[1, 2 * i : 2 * i + 1, c] * keep
            far = halo_r[1, 2 * i + 1 : 2 * i + 2, c] * keep
            x1 = jnp.where(row == LANES - 1, near, pltpu.roll(x, LANES - 1, 0))
            x2 = jnp.where(
                row == LANES - 1,
                far,
                jnp.where(row == LANES - 2, near, pltpu.roll(x, LANES - 2, 0)),
            )
            fgrad_v[i, :, c] = (
                taps[i, 0 : 1, c] * x
                + taps[i, 1 : 2, c] * x1
                + taps[i, 2 : 3, c] * x2
            )
    fgrad_copy = pltpu.make_async_copy(fgrad_v, fgrad, out_sem.at[1])
    fgrad_copy.start()
    arrived(5, land=hgrad)
    out_copy.wait()
    fgrad_copy.wait()

    for u in range(6):
        gone = pl.ds(0, (n_ctx - 1) * CH)
        pltpu.make_async_copy(send.at[u, gone], send.at[u, gone], send_sem.at[u]).wait()
    first_halo.wait_send()
    last_halo.wait_send()
    spent = pl.ds(0, n_ten - 1)
    pltpu.make_async_copy(norm_r.at[spent], norm_r.at[spent], norm_send).wait()


def deliver(a, b, c, a_out, b_out, c_out, a_mid, b_mid, c_mid, c_turned, sem):
    loads = [
        pltpu.make_async_copy(x, y, sem.at[i])
        for i, (x, y) in enumerate(((c, c_mid), (b, b_mid), (a, a_mid)))
    ]
    stores = [
        pltpu.make_async_copy(x, y, sem.at[3 + i])
        for i, (x, y) in enumerate(((c_turned, c_out), (b_mid, b_out), (a_mid, a_out)))
    ]
    for load in loads:
        load.start()
    for load, store in zip(loads, stores):
        load.wait()
        if load is loads[0]:
            for j in range(0, c_mid.shape[0], LANES):
                c_turned[:, j : j + LANES] = c_mid[j : j + LANES, :].T
        store.start()
    for store in stores:
        store.wait()


def per_device(features, short_filter, long_filter, skip_gain, norm_gain, out_grad):
    rows, wide = long_filter.shape
    anywhere = pl.BlockSpec(memory_space=pl.ANY)
    column = pltpu.VMEM((wide, rows), F32)
    spec = pltpu.VMEM((wide, 2 * rows), F32)
    half = pltpu.VMEM((wide, 2 * rows), BF16)
    consts = jnp.asarray(constants(64, rows))
    operands = (
        features,
        short_filter,
        long_filter,
        skip_gain.reshape(1, wide),
        norm_gain.reshape(1, wide),
        out_grad,
        consts,
    )
    shapes = (
        jax.ShapeDtypeStruct((rows, wide), BF16),
        jax.ShapeDtypeStruct((3, rows, wide), F32),
        jax.ShapeDtypeStruct((rows, wide), F32),
    )
    column_grad = jax.ShapeDtypeStruct((wide, rows), F32)
    results = pl.pallas_call(
        kernel,
        out_shape=shapes[:2] + (column_grad,),
        in_specs=[anywhere] * N_IN,
        out_specs=[anywhere] * 3,
        scratch_shapes=[
            pltpu.VMEM((6, wide, rows), F32),
            pltpu.VMEM((6, wide, rows), F32),
        ]
        + [column] * 7
        + [spec] * 3
        + [half] * 2
        + [
            pltpu.VMEM((3, rows, wide), F32),
            pltpu.VMEM((2, 8, wide), F32),
            pltpu.VMEM((2, 8, wide), F32),
            pltpu.VMEM((2, rows), F32),
            pltpu.VMEM((8, 2, rows), F32),
            pltpu.VMEM((256, 64), BF16),
            pltpu.VMEM((256, 256), BF16),
            pltpu.VMEM((256, 256), BF16),
            pltpu.VMEM((64, 128), BF16),
            pltpu.VMEM((64, 128), BF16),
            pltpu.VMEM((256, 256), BF16),
            pltpu.VMEM((256, 256), BF16),
            pltpu.VMEM((64, 128), F32),
            pltpu.VMEM((64, 128), F32),
            pltpu.SemaphoreType.DMA((6,)),
            pltpu.SemaphoreType.DMA((12,)),
            pltpu.SemaphoreType.DMA((2,)),
            pltpu.SemaphoreType.DMA((2,)),
            pltpu.SemaphoreType.DMA,
            pltpu.SemaphoreType.DMA,
            pltpu.SemaphoreType.DMA((N_IN,)),
            pltpu.SemaphoreType.REGULAR,
            pltpu.VMEM((rows, wide), BF16),
            pltpu.VMEM((3, rows, wide), F32),
            pltpu.SemaphoreType.DMA((2,)),
        ]
        + [pltpu.VMEM(x.shape, x.dtype) for x in operands],
        compiler_params=pltpu.CompilerParams(
            collective_id=0, has_side_effects=True, vmem_limit_bytes=VMEM_BYTES
        ),
    )(*operands)
    return pl.pallas_call(
        deliver,
        out_shape=shapes,
        in_specs=[anywhere] * 3,
        out_specs=[anywhere] * 3,
        scratch_shapes=[pltpu.VMEM(x.shape, x.dtype) for x in shapes[:2] + (column_grad, shapes[2])]
        + [pltpu.SemaphoreType.DMA((6,))],
        compiler_params=pltpu.CompilerParams(vmem_limit_bytes=VMEM_BYTES),
    )(*results)


def solution(mesh):
    return jax.shard_map(
        per_device,
        mesh=mesh,
        in_specs=(
            P(None, "context", "tensor"),
            P(None, None, "tensor"),
            P("context", "tensor"),
            P("tensor"),
            P("tensor"),
            P("context", "tensor"),
        ),
        out_specs=(P("context", "tensor"), P(None, "context", "tensor"), P("context", "tensor")),
        check_vma=False,
    )
```

```python
import functools

import jax
import jax.numpy as jnp
import numpy as np
from jax import lax
from jax.experimental import pallas as pl
from jax.experimental.pallas import tpu as pltpu
from jax.sharding import PartitionSpec as P

CHANNELS = 4096
EPS = 1e-06
F32 = jnp.float32
BF16 = jnp.bfloat16
MESH = pl.DeviceIdType.MESH
RING = 16
SIDE = 4
LANES = 128
CH = 8
HALF = CH // 2
N_IN = 7
VMEM_BYTES = 63 * 1024 * 1024


def constants(blocks, width):
    length = 2 * blocks * width
    a = np.arange(blocks)
    k1 = np.arange(blocks) + 0.5
    first = 2.0 * np.pi * k1[:, None] * a[None, :] / (2 * blocks)
    f1 = np.concatenate([np.cos(first), -np.sin(first)], axis=0)
    g1 = np.concatenate([np.cos(first.T), -np.sin(first.T)], axis=1) * (2.0 / length)
    b = np.arange(width)
    twist = 2.0 * np.pi * k1[:, None] * b[None, :] / length
    second = 2.0 * np.pi * ((b[:, None] * b[None, :]) % width) / width
    c, s = np.cos(second), np.sin(second)
    f2 = np.block([[c, -s], [s, c]])
    g2 = np.block([[c, s], [-s, c]])

    pack = np.zeros((6 * width, 2 * width), np.float32)
    pack[: 2 * width] = f2
    pack[2 * width : 4 * width] = g2
    pack[4 * width : 5 * width, :blocks] = f1
    pack[5 * width : 5 * width + blocks, :width] = g1
    pack[5 * width + blocks : 6 * width, :width] = np.cos(twist)
    pack[5 * width + blocks : 6 * width, width:] = np.sin(twist)
    return pack


def dot(a, b):
    return jnp.dot(a, b, preferred_element_type=F32)


def halves(x):
    high = x.astype(BF16)
    return high, (x - high.astype(F32)).astype(BF16)


def kernel(
    *refs,
):
    held, (out, fgrad, hgrad) = refs[:N_IN], refs[N_IN : N_IN + 3]
    (send, recv, qt, kt, vt, st, it, gt, ct, spec_h, spec_x, spec_g, th, tl, db,
     halo_s, halo_r, norm_s, norm_r,
     f1, f2h, f2l, g1h, g1l, g2h, g2l, wr, wi,
     send_sem, recv_sem, halo_send, halo_recv, norm_send, norm_recv, in_sem, ring_sem,
     out_v, fgrad_v, out_sem) = refs[N_IN + 3 : -N_IN]
    local = refs[-N_IN:]
    feat, taps, filt, skip, gain, grad, consts = local
    fetch = [
        pltpu.make_async_copy(held[i], local[i], in_sem.at[i]) for i in range(N_IN)
    ]
    early = (2, 0)
    late = [i for i in range(N_IN) if i not in early]
    for i in early:
        fetch[i].start()
    me = lax.axis_index("context")
    lane = lax.axis_index("tensor")
    n_ctx = lax.axis_size("context")
    n_ten = lax.axis_size("tensor")
    my_z, my_y = me // SIDE, me % SIDE
    wide = LANES * SIDE
    chunks = [slice(j * LANES, (j + 1) * LANES) for j in range(wide // LANES)]

    columns = [(my_y + i) % SIDE for i in (2, 1, 3, 0)]

    def ring_row(j):
        k = RING - 1 - j
        odd = (k + lane) % 2
        m = k // 2 + k % 2
        dz = odd * m + (1 - odd) * (RING - m)
        return ((my_z + dz) % RING) * SIDE

    barrier = pltpu.get_barrier_semaphore()

    def greet_z(i, carry):
        p = ((my_z + i) % RING) * SIDE + my_y
        pl.semaphore_signal(barrier, inc=1, device_id={"context": p}, device_id_type=MESH)
        return carry

    def greet_tensor(i, carry):
        pl.semaphore_signal(
            barrier, inc=1, device_id={"tensor": (lane + i) % n_ten}, device_id_type=MESH
        )
        return carry

    beside = [my_z * SIDE + (my_y + i) % SIDE for i in range(1, SIDE)]
    lax.fori_loop(1, RING, greet_z, 0)
    for p in beside:
        pl.semaphore_signal(barrier, inc=1, device_id={"context": p}, device_id_type=MESH)
    lax.fori_loop(1, n_ten, greet_tensor, 0)
    for i in late:
        fetch[i].start()

    def piece(i, part):
        if part is None:
            return pl.ds(pl.multiple_of(i * CH, CH), CH)
        return pl.ds(pl.multiple_of(i * CH + part * HALF, HALF), HALF)

    def scatter(u, part=None, land=None, first=0):
        slot = 2 * u + (part or 0)
        land = recv.at[u] if land is None else land
        mine = piece(me, part)
        pltpu.make_async_copy(send.at[u, mine], land.at[mine], recv_sem.at[slot]).start()

        def push(p):
            pltpu.make_async_remote_copy(
                src_ref=send.at[u, piece(p, part)],
                dst_ref=land.at[mine],
                send_sem=send_sem.at[u],
                recv_sem=recv_sem.at[slot],
                device_id={"context": p},
                device_id_type=MESH,
            ).start()

        def body(j, carry):
            row = ring_row(j)
            if first:

                @pl.when(row >= first * SIDE)
                def _():
                    for y in columns:
                        push(row + y)

            else:
                for y in columns:
                    push(row + y)
            return carry

        def ahead(i, carry):
            row = ((i + my_z) % first) * SIDE
            for y in columns:

                @pl.when(row + y != me)
                def _():
                    push(row + y)

            return carry

        def own_row():
            for y in columns[:-1]:
                push(my_z * SIDE + y)

        if first:
            lax.fori_loop(0, first, ahead, 0)
        lax.fori_loop(0, RING - 1, body, 0)
        if first:
            pl.when(my_z >= first)(own_row)
        else:
            own_row()

    def arrived(u, part=None, land=None):
        slot = 2 * u + (part or 0)
        land = recv.at[u] if land is None else land
        size = pl.ds(0, n_ctx * (CH if part is None else HALF))
        pltpu.make_async_copy(send.at[u, size], land.at[size], recv_sem.at[slot]).wait()

    def halo_copy(h, to):
        return pltpu.make_async_remote_copy(
            src_ref=halo_s.at[h],
            dst_ref=halo_r.at[h],
            send_sem=halo_send.at[h],
            recv_sem=halo_recv.at[h],
            device_id={"context": to},
            device_id_type=MESH,
        )

    fetch[2].wait()
    for j, c in enumerate(chunks):
        send[0, c, :] = filt[:, c].astype(F32).T
    fetch[0].wait()
    for i in range(3):
        halo_s[0, 2 * i : 2 * i + 2, :] = feat[i, 112:128, :].astype(F32)[14:16]
    halo_s[0, 6:8, :] = jnp.zeros((2, wide), F32)
    pl.semaphore_wait(barrier, RING - 1 + SIDE - 1 + n_ten - 1)
    for p in beside:
        pl.semaphore_signal(ring_sem, inc=1, device_id={"context": p}, device_id_type=MESH)
    pl.semaphore_wait(ring_sem, SIDE - 1)

    first_halo = halo_copy(0, (me + 1) % n_ctx)
    first_halo.start()
    scatter(0)
    for i in late:
        fetch[i].wait()
    f2h[...], f2l[...] = halves(consts[0:256, :])
    g2h[...], g2l[...] = halves(consts[256:512, :])
    f1[0:128, :], f1[128:256, :] = halves(consts[512:640, 0:64])
    g1h[...], g1l[...] = halves(consts[640:704, 0:128])
    wr[...] = consts[704:768, 0:128]
    wi[...] = consts[704:768, 128:256]

    for j, c in enumerate(chunks):
        st[c, :] = (grad[:, c].astype(F32) * gain[0:1, c]).T
        gt[c, :] = jnp.broadcast_to(skip[0:1, c], (LANES, LANES)).T

    row = lax.broadcasted_iota(jnp.int32, (LANES, LANES), 0)
    first_halo.wait_recv()
    keep = (me > 0).astype(F32)
    for j, c in enumerate(chunks):
        parts = []
        for i in range(3):
            x = feat[i, :, c].astype(F32)
            far = halo_r[0, 2 * i : 2 * i + 1, c] * keep
            near = halo_r[0, 2 * i + 1 : 2 * i + 2, c] * keep
            x1 = jnp.where(row == 0, near, pltpu.roll(x, 1, 0))
            x2 = jnp.where(row == 0, far, jnp.where(row == 1, near, pltpu.roll(x, 2, 0)))
            parts.append(
                taps[i, 0 : 1, c] * x
                + taps[i, 1 : 2, c] * x1
                + taps[i, 2 : 3, c] * x2
            )
        qt[c, :] = parts[0].T
        k, v = parts[1].T, parts[2].T
        kt[c, :] = k
        vt[c, :] = v
        send[1, c, :] = (k * v).astype(BF16).astype(F32)
    scatter(1, 0)
    scatter(1, 1)

    blocks = 64

    def forward(u, spec, part):
        for p in range(part * HALF // 2, (part + 1) * HALF // 2):
            x = jnp.concatenate(
                [recv[u, pl.ds(2 * p + e, blocks, stride=CH), :] for e in range(2)], axis=1
            ).astype(BF16)
            z = dot(f1[...], x)
            z = z[: 2 * blocks] + z[2 * blocks :]
            for e in range(2):
                re = z[:blocks, e * LANES : (e + 1) * LANES]
                im = z[blocks:, e * LANES : (e + 1) * LANES]
                rows = slice((2 * p + e) * blocks, (2 * p + e + 1) * blocks)
                h, l = halves(re * wr[...] + im * wi[...])
                th[rows, :LANES] = h
                tl[rows, :LANES] = l
                h, l = halves(im * wr[...] - re * wi[...])
                th[rows, LANES:] = h
                tl[rows, LANES:] = l
        rows = slice(part * HALF * blocks, (part + 1) * HALF * blocks)
        spec[rows, :] = dot(th[rows, :], f2h[...]) + dot(tl[rows, :], f2h[...]) + dot(th[rows, :], f2l[...])

    def inverse(a, b, sign, u, part):
        for p in range(part * HALF // 2, (part + 1) * HALF // 2):
            rows = slice(2 * p * blocks, 2 * (p + 1) * blocks)
            ar, ai = a[rows, :LANES], a[rows, LANES:]
            br, bi = b[rows, :LANES], sign * b[rows, LANES:]
            h, l = halves(ar * br - ai * bi)
            th[rows, :LANES] = h
            tl[rows, :LANES] = l
            h, l = halves(ar * bi + ai * br)
            th[rows, LANES:] = h
            tl[rows, LANES:] = l
        base = part * HALF * blocks
        rows = slice(base, base + HALF * blocks)
        t = dot(th[rows, :], g2h[...]) + dot(tl[rows, :], g2h[...]) + dot(th[rows, :], g2l[...])
        for p in range(part * HALF // 2, (part + 1) * HALF // 2):
            both = []
            for e in range(2):
                rows = slice((2 * p + e) * blocks - base, (2 * p + e + 1) * blocks - base)
                re, im = t[rows, :LANES], t[rows, LANES:]
                both.append(
                    jnp.concatenate(
                        [re * wr[...] - im * wi[...], im * wr[...] + re * wi[...]], axis=0
                    )
                )
            h, l = halves(jnp.concatenate(both, axis=1))
            y = dot(g1h[...], h) + dot(g1h[...], l) + dot(g1l[...], h)
            for e in range(2):
                send[u, pl.ds(2 * p + e, blocks, stride=CH), :] = y[:, e * LANES : (e + 1) * LANES]

    arrived(0)
    for part in range(2):
        forward(0, spec_h, part)
    for part in range(2):
        arrived(1, part)
        forward(1, spec_x, part)
        inverse(spec_x, spec_h, 1.0, 2, part)
        scatter(2, part)

    for part in range(2):
        arrived(2, part)
    square = jnp.zeros((1, LANES), F32)
    cross = jnp.zeros((1, LANES), F32)
    for c in chunks:
        inner = recv[2, c, :] + gt[c, :] * send[1, c, :]
        gated = qt[c, :] * inner
        ct[c, :] = gated
        square = square + jnp.sum(gated * gated, axis=0, keepdims=True)
        cross = cross + jnp.sum(st[c, :] * gated, axis=0, keepdims=True)
    norm_s[0:1, :] = square
    norm_s[1:2, :] = cross
    pltpu.make_async_copy(norm_s, norm_r.at[lane], norm_recv).start()

    for i in (4, 5, 3, 6, 2, 7, 1):
        pltpu.make_async_remote_copy(
            src_ref=norm_s,
            dst_ref=norm_r.at[lane],
            send_sem=norm_send,
            recv_sem=norm_recv,
            device_id={"tensor": (lane + i) % n_ten},
            device_id_type=MESH,
        ).start()
    pltpu.make_async_copy(norm_r, norm_r, norm_recv).wait()
    total = norm_r[0]
    for i in range(1, 8):
        total = total + norm_r[i]
    scale = lax.rsqrt(total[0:1] / CHANNELS + EPS)
    pull = scale * scale * scale * (total[1:2] / CHANNELS)
    for c in chunks:
        d_gated = scale * st[c, :] - ct[c, :] * pull
        send[3, c, :] = (d_gated * qt[c, :]).astype(BF16).astype(F32)
    scatter(3, 0)
    scatter(3, 1)
    for c in chunks:
        d_gated = scale * st[c, :] - ct[c, :] * pull
        it[c, :] = d_gated * (recv[2, c, :] + gt[c, :] * send[1, c, :])
        gt[c, :] = gt[c, :] * (d_gated * qt[c, :])
    for c in chunks:
        out_v[:, c] = ((ct[c, :] * scale).T * gain[0:1, c]).astype(BF16)
        db[0, :, c] = it[c, :].T

    out_copy = pltpu.make_async_copy(out_v, out, out_sem.at[0])
    out_copy.start()
    for part in range(2):
        arrived(3, part)
        forward(3, spec_g, part)
        inverse(spec_g, spec_h, -1.0, 4, part)
        scatter(4, part)
        inverse(spec_g, spec_x, -1.0, 5, part)
    scatter(5, land=hgrad, first=4)
    for part in range(2):
        arrived(4, part)
    for c in chunks:
        d_mixed = recv[4, c, :] + gt[c, :]
        db[1, :, c] = (d_mixed * vt[c, :]).T
        db[2, :, c] = (d_mixed * kt[c, :]).T
    for i in range(3):
        halo_s[1, 2 * i : 2 * i + 2, :] = db[i, 0:2, :]
    halo_s[1, 6:8, :] = jnp.zeros((2, wide), F32)
    last_halo = halo_copy(1, (me + n_ctx - 1) % n_ctx)
    last_halo.start()
    last_halo.wait_recv()
    keep = (me < n_ctx - 1).astype(F32)
    for c in chunks:
        for i in range(3):
            x = db[i, :, c]
            near = halo_r[1, 2 * i : 2 * i + 1, c] * keep
            far = halo_r[1, 2 * i + 1 : 2 * i + 2, c] * keep
            x1 = jnp.where(row == LANES - 1, near, pltpu.roll(x, LANES - 1, 0))
            x2 = jnp.where(
                row == LANES - 1,
                far,
                jnp.where(row == LANES - 2, near, pltpu.roll(x, LANES - 2, 0)),
            )
            fgrad_v[i, :, c] = (
                taps[i, 0 : 1, c] * x
                + taps[i, 1 : 2, c] * x1
                + taps[i, 2 : 3, c] * x2
            )
    fgrad_copy = pltpu.make_async_copy(fgrad_v, fgrad, out_sem.at[1])
    fgrad_copy.start()
    arrived(5, land=hgrad)
    out_copy.wait()
    fgrad_copy.wait()

    for u in range(6):
        gone = pl.ds(0, (n_ctx - 1) * CH)
        pltpu.make_async_copy(send.at[u, gone], send.at[u, gone], send_sem.at[u]).wait()
    first_halo.wait_send()
    last_halo.wait_send()
    spent = pl.ds(0, n_ten - 1)
    pltpu.make_async_copy(norm_r.at[spent], norm_r.at[spent], norm_send).wait()


def deliver(a, b, c, a_out, b_out, c_out, a_mid, b_mid, c_mid, c_turned, sem):
    loads = [
        pltpu.make_async_copy(x, y, sem.at[i])
        for i, (x, y) in enumerate(((c, c_mid), (b, b_mid), (a, a_mid)))
    ]
    stores = [
        pltpu.make_async_copy(x, y, sem.at[3 + i])
        for i, (x, y) in enumerate(((c_turned, c_out), (b_mid, b_out), (a_mid, a_out)))
    ]
    for load in loads:
        load.start()
    for load, store in zip(loads, stores):
        load.wait()
        if load is loads[0]:
            for j in range(0, c_mid.shape[0], LANES):
                c_turned[:, j : j + LANES] = c_mid[j : j + LANES, :].T
        store.start()
    for store in stores:
        store.wait()


def per_device(features, short_filter, long_filter, skip_gain, norm_gain, out_grad):
    rows, wide = long_filter.shape
    anywhere = pl.BlockSpec(memory_space=pl.ANY)
    column = pltpu.VMEM((wide, rows), F32)
    spec = pltpu.VMEM((wide, 2 * rows), F32)
    half = pltpu.VMEM((wide, 2 * rows), BF16)
    consts = jnp.asarray(constants(64, rows))
    operands = (
        features,
        short_filter,
        long_filter,
        skip_gain.reshape(1, wide),
        norm_gain.reshape(1, wide),
        out_grad,
        consts,
    )
    shapes = (
        jax.ShapeDtypeStruct((rows, wide), BF16),
        jax.ShapeDtypeStruct((3, rows, wide), F32),
        jax.ShapeDtypeStruct((rows, wide), F32),
    )
    column_grad = jax.ShapeDtypeStruct((wide, rows), F32)
    results = pl.pallas_call(
        kernel,
        out_shape=shapes[:2] + (column_grad,),
        in_specs=[anywhere] * N_IN,
        out_specs=[anywhere] * 3,
        scratch_shapes=[
            pltpu.VMEM((6, wide, rows), F32),
            pltpu.VMEM((6, wide, rows), F32),
        ]
        + [column] * 7
        + [spec] * 3
        + [half] * 2
        + [
            pltpu.VMEM((3, rows, wide), F32),
            pltpu.VMEM((2, 8, wide), F32),
            pltpu.VMEM((2, 8, wide), F32),
            pltpu.VMEM((2, rows), F32),
            pltpu.VMEM((8, 2, rows), F32),
            pltpu.VMEM((256, 64), BF16),
            pltpu.VMEM((256, 256), BF16),
            pltpu.VMEM((256, 256), BF16),
            pltpu.VMEM((64, 128), BF16),
            pltpu.VMEM((64, 128), BF16),
            pltpu.VMEM((256, 256), BF16),
            pltpu.VMEM((256, 256), BF16),
            pltpu.VMEM((64, 128), F32),
            pltpu.VMEM((64, 128), F32),
            pltpu.SemaphoreType.DMA((6,)),
            pltpu.SemaphoreType.DMA((12,)),
            pltpu.SemaphoreType.DMA((2,)),
            pltpu.SemaphoreType.DMA((2,)),
            pltpu.SemaphoreType.DMA,
            pltpu.SemaphoreType.DMA,
            pltpu.SemaphoreType.DMA((N_IN,)),
            pltpu.SemaphoreType.REGULAR,
            pltpu.VMEM((rows, wide), BF16),
            pltpu.VMEM((3, rows, wide), F32),
            pltpu.SemaphoreType.DMA((2,)),
        ]
        + [pltpu.VMEM(x.shape, x.dtype) for x in operands],
        compiler_params=pltpu.CompilerParams(
            collective_id=0, has_side_effects=True, vmem_limit_bytes=VMEM_BYTES
        ),
    )(*operands)
    return pl.pallas_call(
        deliver,
        out_shape=shapes,
        in_specs=[anywhere] * 3,
        out_specs=[anywhere] * 3,
        scratch_shapes=[pltpu.VMEM(x.shape, x.dtype) for x in shapes[:2] + (column_grad, shapes[2])]
        + [pltpu.SemaphoreType.DMA((6,))],
        compiler_params=pltpu.CompilerParams(vmem_limit_bytes=VMEM_BYTES),
    )(*results)


def solution(mesh):
    return jax.shard_map(
        per_device,
        mesh=mesh,
        in_specs=(
            P(None, "context", "tensor"),
            P(None, None, "tensor"),
            P("context", "tensor"),
            P("tensor"),
            P("tensor"),
            P("context", "tensor"),
        ),
        out_specs=(P("context", "tensor"), P(None, "context", "tensor"), P("context", "tensor")),
        check_vma=False,
    )
```
